256 devices in a mesh: dp: 8 (over x_lo, y), ctx: 32 (over z, x_hi, core).
Axes of the slice: x: 4 (x_hi: 2, x_lo: 2; x = x_hi * 2 + x_lo), y: 4, z: 8, core: 2. Of those that a mesh axis runs over, the one named last changes fastest.
Arguments:
- queries: bfloat16 [65536, 128], P(('dp', 'ctx')), parts along dimension 0, may hold values from -6 to 6
- key_rows: bfloat16 [65536, 128], P(('dp', 'ctx')), parts along dimension 0, may hold values from -6 to 6
- value_rows: bfloat16 [65536, 128], P(('dp', 'ctx')), parts along dimension 0, may hold values from -0.5 to 0.5
- out_grad: bfloat16 [65536, 128], P(('dp', 'ctx')), parts along dimension 0, may hold values from -6 to 6
Outputs:
- query_grad: float32 [65536, 128], P(('dp', 'ctx')), parts along dimension 0
- key_grad: float32 [65536, 128], P(('dp', 'ctx')), parts along dimension 0
- value_grad: float32 [65536, 128], P(('dp', 'ctx')), parts along dimension 0
The draws below stay inside these ranges and needn't reach their ends.
There are 8 independent parts, one for each index of `dp`. The reference program is written for one: setup_inputs(seed, part) draws one part's arguments, and reference() takes and returns one part's arrays. A program takes and returns all parts, laid end to end along the dimension named above; each array names one. Nothing has to cross between parts.
All inputs are finite; a program needn't handle non-finite values.
Results may differ from the reference program's by a relative error of at most 0.0069.
Values may be sent and summed in bfloat16 or wider, within the bound.
A program may use at most 64 MiB of HBM per device.

```python
import jax
import jax.numpy as jnp
from jax import lax

DH = 128
TOK_DEV = 256
SEQ = 8192


def drawn_pair(key):
    query_key = jax.random.fold_in(key, 101)
    other_key = jax.random.fold_in(key, 202)
    query_draw = jnp.clip(1.6 * jax.random.normal(query_key, (SEQ, DH), jnp.float32), -6.0, 6.0)
    key_draw = jnp.clip(1.6 * jax.random.normal(other_key, (SEQ, DH), jnp.float32), -6.0, 6.0)
    return (query_draw, key_draw)


def draw_queries(key, part):
    return drawn_pair(key)[0].astype(jnp.bfloat16)


def draw_key_rows(key, part):
    return drawn_pair(key)[1].astype(jnp.bfloat16)


def shard_levels(own_key, shape, shards, low, largest):
    loudness = 1.0
    for position, blocks in shards:
        heights = jax.random.uniform(jax.random.fold_in(jax.random.fold_in(own_key, 6), position), (blocks,), jnp.float32, low / len(shards), largest / len(shards))
        loudness = loudness * jnp.repeat(jnp.exp(heights), shape[position] // blocks).reshape((-1,) + (1,) * (len(shape) - 1 - position))
    return loudness


def scatter_about(stream_key, extent, deviation, most, pieces=(), held_as=jnp.bfloat16):
    drawn = deviation * jax.random.normal(stream_key, extent, jnp.float32)
    if pieces:
        drawn = drawn * shard_levels(stream_key, extent, pieces, -0.22, 0.18)
    return jnp.clip(drawn, -most, most).astype(held_as)


def setup_inputs(seed: int = 0, part: int = 0) -> dict:
    key_of = jax.random.split(jax.random.key(seed), 5)
    part_splits = jax.random.split(jax.random.fold_in(key_of[4], part), 5)
    queries = draw_queries(jax.random.fold_in(jax.random.fold_in(key_of[4], part), 71), part)
    key_rows = draw_key_rows(jax.random.fold_in(jax.random.fold_in(key_of[4], part), 71), part)
    value_rows = scatter_about(part_splits[2], (SEQ, DH), DH ** -0.5, 0.5, ((0, 32),))
    out_grad = scatter_about(part_splits[3], (SEQ, DH), 1.0, 6.0, ((0, 32),))
    return {"queries": queries, "key_rows": key_rows, "value_rows": value_rows, "out_grad": out_grad}


def reference(queries, key_rows, value_rows, out_grad):
    score_scale = DH ** -0.5
    blocks = SEQ // TOK_DEV
    query_blocks = queries.reshape(blocks, TOK_DEV, DH)
    grad_blocks = out_grad.reshape(blocks, TOK_DEV, DH)

    def one_block(carried, inputs):
        key_grad, value_grad = carried
        query_part, grad_part = inputs
        scores = jnp.dot(query_part, key_rows.T, preferred_element_type=jnp.float32) * score_scale
        prob_grad = jnp.dot(grad_part, value_rows.T, preferred_element_type=jnp.float32)
        row_peak = jnp.max(scores, axis=1)
        weights_now = jnp.exp(scores - row_peak[:, None])
        row_total = jnp.sum(weights_now, axis=1)
        log_total = row_peak + jnp.log(row_total)
        delta = jnp.sum(weights_now * prob_grad, axis=1) / row_total
        probs = jnp.exp(scores - log_total[:, None])
        score_grad = (probs * (prob_grad - delta[:, None])).astype(jnp.bfloat16)
        prob_half = probs.astype(jnp.bfloat16)
        query_grad = jnp.dot(score_grad, key_rows, preferred_element_type=jnp.float32) * score_scale
        key_grad = key_grad + jnp.dot(score_grad.T, query_part, preferred_element_type=jnp.float32)
        value_grad = value_grad + jnp.dot(prob_half.T, grad_part, preferred_element_type=jnp.float32)
        return (key_grad, value_grad), query_grad

    zero_grads = jnp.zeros((SEQ, DH), jnp.float32)
    (key_grad, value_grad), query_grad = lax.scan(one_block, (zero_grads, zero_grads), (query_blocks, grad_blocks))
    return query_grad.reshape(SEQ, DH), key_grad * score_scale, value_grad
```

```python
import math

import jax
import jax.numpy as jnp
from jax import lax
from jax.experimental import pallas as pl
from jax.experimental.pallas import tpu as pltpu
from jax.sharding import PartitionSpec as P

F32 = jnp.float32
BF16 = jnp.bfloat16
MESH = pl.DeviceIdType.MESH

ROWS = 256
WIDTH = 128
RING = 8
HALF = 512
KEYS = 1024
SCALE = WIDTH ** (-0.5)
EXP2_SCALE = SCALE * math.log2(math.e)

OWN, FAR, R1, L1, R2, L2, R3, L3 = range(8)
PLACE = (0, 4, -1, 1, -2, 2, -3, 3)
MIRROR = (OWN, FAR, L1, R1, L2, R2, L3, R3)


def rows_dot(left, right):
    return lax.dot_general(left, right, (((1,), (1,)), ((), ())), preferred_element_type=F32)


def kernel(
    q_hbm, k_hbm, v_hbm, g_hbm,
    dq_hbm, dk_hbm, dv_hbm,
    qbuf, gbuf, kbuf, vbuf, ktbuf, ebuf, dbuf, mbuf,
    part_tx, part_rx, fin, dk_acc, dv_acc,
    dqt, dq_tx, dq_rx, pair_tx, pair_rx, far_tx, far_rx, out_buf,
    in_sem, gat_send, gat_recv, kv_send, kv_recv, st_send, st_recv, fin_send, fin_recv,
    dq_send, dq_recv, red_send, red_recv, out_sem,
):
    me = lax.axis_index("ctx")
    z = me // 4
    w = me % 4
    core = w % 2
    xh = w // 2

    def on_ring(offset):
        return {"ctx": ((z + (offset + RING)) % RING) * 4 + w}

    sibling = {"ctx": z * 4 + xh * 2 + (1 - core)}
    across = {"ctx": z * 4 + (1 - xh) * 2 + core}

    barrier = pltpu.get_barrier_semaphore()
    for peer in [on_ring(PLACE[s]) for s in range(1, 8)] + [sibling, across]:
        pl.semaphore_signal(barrier, inc=1, device_id=peer, device_id_type=MESH)

    own_rows = pl.ds(0, ROWS)
    loads = [
        pltpu.make_async_copy(src, dst, in_sem.at[i])
        for i, (src, dst) in enumerate(
            (
                (q_hbm, qbuf.at[OWN]),
                (g_hbm, gbuf.at[OWN]),
                (k_hbm, kbuf.at[own_rows]),
                (v_hbm, vbuf.at[own_rows]),
            )
        )
    ]
    for c in loads:
        c.start()
    pending = []

    def send(src, dst, send_sem, recv_sem, peer):
        c = pltpu.make_async_remote_copy(
            src_ref=src, dst_ref=dst, send_sem=send_sem, recv_sem=recv_sem,
            device_id=peer, device_id_type=MESH,
        )
        c.start()
        pending.append(c)
        return c

    for c in loads:
        c.wait()
    pl.semaphore_wait(barrier, 9)

    right, left = on_ring(1), on_ring(-1)

    bufs = (qbuf, gbuf)

    def hop(b, d, i):
        slots = ((OWN, R1, R2, R3, FAR), (OWN, L1, L2, L3, FAR))[d]
        n = (b * 2 + d) * 4 + i
        return send(
            bufs[b].at[slots[i]], bufs[b].at[slots[i + 1]],
            gat_send.at[n], gat_recv.at[n], (right, left)[d],
        )

    def key_rows_at(p):
        return pl.ds(p * ROWS, ROWS)

    hops = {}
    for b in (0, 1):
        for d in (0, 1):
            hops[b, d, 0] = hop(b, d, 0)
    kv_across = []
    for i, buf in enumerate((kbuf, vbuf)):
        kv_across.append(
            send(buf.at[key_rows_at(0)], buf.at[key_rows_at(2)], kv_send.at[i], kv_recv.at[i], across)
        )
    kv_sibling = []
    for i, buf in enumerate((kbuf, vbuf)):
        kv_sibling.append(
            send(buf.at[key_rows_at(0)], buf.at[key_rows_at(1)], kv_send.at[2 + i], kv_recv.at[2 + i], sibling)
        )
    kv_third = []

    def pass_keys_on():
        for i, buf in enumerate((kbuf, vbuf)):
            kv_across[i].wait_recv()
            kv_third.append(
                send(buf.at[key_rows_at(2)], buf.at[key_rows_at(3)], kv_send.at[4 + i], kv_recv.at[4 + i], sibling)
            )

    def tile(slot, kh):
        keys = pl.ds(kh * HALF, HALF)
        s = rows_dot(kbuf[keys, :], qbuf[slot])
        m = jnp.max(s, axis=0, keepdims=True)
        e = jnp.exp2((s - m) * EXP2_SCALE)
        ebuf[slot, keys, :] = e
        d = rows_dot(vbuf[keys, :], gbuf[slot])
        dbuf[slot, keys, :] = d
        mbuf[slot, kh, 0:1, :] = m * SCALE
        mbuf[slot, kh, 1:2, :] = jnp.sum(e, axis=0, keepdims=True)
        mbuf[slot, kh, 2:3, :] = jnp.sum(e * d, axis=0, keepdims=True)

    def put_stats(ref, log_total, delta):
        for i in range(2):
            cols = slice(i * 128, (i + 1) * 128)
            ref[i : i + 1, :] = log_total[:, cols]
            ref[2 + i : 3 + i, :] = delta[:, cols]

    st = {}

    def stats(slot):
        m0, l0, w0 = (mbuf[slot, 0, i : i + 1, :] for i in range(3))
        m1, l1, w1 = (mbuf[slot, 1, i : i + 1, :] for i in range(3))
        m = jnp.maximum(m0, m1)
        a0, a1 = jnp.exp(m0 - m), jnp.exp(m1 - m)
        total = l0 * a0 + l1 * a1
        put_stats(part_tx.at[slot], m + jnp.log(total), (w0 * a0 + w1 * a1) / total)
        if slot != OWN:
            at = MIRROR[slot]
            st[slot] = send(
                part_tx.at[slot], part_rx.at[at], st_send.at[slot], st_recv.at[at], on_ring(PLACE[slot])
            )

    def wait_gather(b, i):
        hops[b, 0, i].wait_recv()
        if i < 3 or b == 0:
            pass

    def arrive(b, i):
        for d in (0, 1):
            hops[b, d, i].wait_recv()
            if i < 2 or b == d:
                hops[b, d, i + 1] = hop(b, d, i + 1)

    for c in kv_sibling:
        c.wait_recv()
    tile(OWN, 0)
    arrive(0, 0)
    arrive(1, 0)
    tile(R1, 0)
    tile(L1, 0)
    pass_keys_on()
    arrive(0, 1)
    for c in kv_third:
        c.wait_recv()
    for p in range(4):
        ktbuf[:, p * ROWS : (p + 1) * ROWS] = kbuf[key_rows_at(p), :].astype(F32).T.astype(BF16)
    tile(OWN, 1)
    stats(OWN)
    arrive(1, 1)
    for slot in (R1, L1):
        tile(slot, 1)
        stats(slot)
    for slot in (R2, L2):
        tile(slot, 0)
        tile(slot, 1)
        stats(slot)
    arrive(0, 2)
    arrive(1, 2)
    for slot in (R3, L3):
        tile(slot, 0)
        tile(slot, 1)
        stats(slot)
    hops[0, 0, 3].wait_recv()
    hops[1, 1, 3].wait_recv()
    tile(FAR, 0)
    tile(FAR, 1)
    stats(FAR)

    order = (OWN, R1, L1, R2, L2, R3, L3, FAR)
    parts = []
    for slot in order:
        if slot == OWN:
            parts.append((part_tx[OWN, 0:2, :], part_tx[OWN, 2:4, :]))
        else:
            pltpu.make_async_remote_copy(
                src_ref=part_tx.at[slot], dst_ref=part_rx.at[slot],
                send_sem=st_send.at[slot], recv_sem=st_recv.at[slot],
                device_id=on_ring(PLACE[slot]), device_id_type=MESH,
            ).wait_recv()
            parts.append((part_rx[slot, 0:2, :], part_rx[slot, 2:4, :]))
    peak = parts[0][0]
    for log_part, _ in parts[1:]:
        peak = jnp.maximum(peak, log_part)
    total = jnp.zeros_like(peak)
    weighted = jnp.zeros_like(peak)
    for log_part, delta_part in parts:
        share = jnp.exp(log_part - peak)
        total = total + share
        weighted = weighted + share * delta_part
    fin[OWN, 0:2, :] = peak + jnp.log(total)
    fin[OWN, 2:4, :] = weighted / total
    fin_copies = {}
    for slot in (FAR, R3, L3, R2, L2, R1, L1):
        at = MIRROR[slot]
        fin_copies[at] = send(
            fin.at[OWN], fin.at[at], fin_send.at[slot], fin_recv.at[at], on_ring(PLACE[slot])
        )

    first = [True]

    def grads(slot):
        if slot != OWN:
            fin_copies[slot].wait_recv()
        log_total = jnp.concatenate([fin[slot, 0:1, :], fin[slot, 1:2, :]], axis=1)
        delta = jnp.concatenate([fin[slot, 2:3, :], fin[slot, 3:4, :]], axis=1)
        dq_t = None
        for kh in range(2):
            keys = pl.ds(kh * HALF, HALF)
            c = jnp.exp(mbuf[slot, kh, 0:1, :] - log_total)
            p = ebuf[slot, keys, :] * c
            prob_half = p.astype(BF16)
            score_grad = (p * (dbuf[slot, keys, :] - delta)).astype(BF16)
            dv = jnp.dot(prob_half, gbuf[slot], preferred_element_type=F32)
            dk = jnp.dot(score_grad, qbuf[slot], preferred_element_type=F32)
            if first[0]:
                dv_acc[keys, :] = dv
                dk_acc[keys, :] = dk
            else:
                dv_acc[keys, :] += dv
                dk_acc[keys, :] += dk
            t = jnp.dot(ktbuf[:, keys], score_grad, preferred_element_type=F32)
            dq_t = t if dq_t is None else dq_t + t
        first[0] = False
        return dq_t

    dq = {}

    def pass_sum(d, i, rows):
        n = d * 4 + i
        dq[d, i] = send(
            dq_tx.at[n, rows], dq_rx.at[n, rows], dq_send.at[n], dq_recv.at[n], (left, right)[d]
        )

    halves = (pl.ds(0, 64), pl.ds(64, 64))
    t = grads(FAR)
    dq_tx[0, 0:64, :] = t[0:64].astype(BF16)
    pass_sum(0, 0, halves[0])
    dq_tx[4, 64:128, :] = t[64:128].astype(BF16)
    pass_sum(1, 0, halves[1])
    for i, pair in enumerate(((R3, L3), (R2, L2), (R1, L1))):
        for d in (0, 1):
            t = grads(pair[d])
            dq[d, i].wait_recv()
            n = d * 4 + i
            if i == 0:
                dqt[...] = t
                dqt[halves[d], :] += dq_rx[n, halves[d], :].astype(F32)
                t = dqt[...]
            else:
                t = t + dq_rx[n].astype(F32)
            dq_tx[n + 1] = t.astype(BF16)
            pass_sum(d, i + 1, pl.ds(0, 128))
    dqt[...] = grads(OWN)

    red = []
    for j, p in enumerate((3, 1)):
        pair_tx[j, 0] = dk_acc[key_rows_at(p), :].astype(BF16)
        pair_tx[j, 1] = dv_acc[key_rows_at(p), :].astype(BF16)
        red.append(send(pair_tx.at[j], pair_rx.at[j], red_send.at[j], red_recv.at[j], sibling))
    red[0].wait_recv()
    far_tx[0] = (dk_acc[key_rows_at(2), :] + pair_rx[0, 0].astype(F32)).astype(BF16)
    far_tx[1] = (dv_acc[key_rows_at(2), :] + pair_rx[0, 1].astype(F32)).astype(BF16)
    red.append(send(far_tx, far_rx, red_send.at[2], red_recv.at[2], across))

    dq[0, 3].wait_recv()
    dq[1, 3].wait_recv()
    t = dqt[...] + dq_rx[3].astype(F32) + dq_rx[7].astype(F32)
    out_buf[0] = t.T * SCALE
    outs = [pltpu.make_async_copy(out_buf.at[0], dq_hbm, out_sem.at[0])]
    outs[0].start()
    red[1].wait_recv()
    red[2].wait_recv()
    for i, (acc, out, scale) in enumerate(((dk_acc, dk_hbm, SCALE), (dv_acc, dv_hbm, None))):
        t = acc[key_rows_at(0), :] + pair_rx[1, i].astype(F32) + far_rx[i].astype(F32)
        out_buf[1 + i] = t if scale is None else t * scale
        c = pltpu.make_async_copy(out_buf.at[1 + i], out, out_sem.at[1 + i])
        c.start()
        outs.append(c)
    for c in pending:
        c.wait_send()
    for c in outs:
        c.wait()


def shards(queries, key_rows, value_rows, out_grad):
    any_spec = pl.BlockSpec(memory_space=pl.ANY)
    dma = pltpu.SemaphoreType.DMA
    out = jax.ShapeDtypeStruct((ROWS, WIDTH), F32)
    vm = pltpu.VMEM
    return pl.pallas_call(
        kernel,
        out_shape=(out, out, out),
        in_specs=[any_spec] * 4,
        out_specs=(any_spec,) * 3,
        scratch_shapes=[
            vm((8, ROWS, WIDTH), BF16),
            vm((8, ROWS, WIDTH), BF16),
            vm((KEYS, WIDTH), BF16),
            vm((KEYS, WIDTH), BF16),
            vm((WIDTH, KEYS), BF16),
            vm((8, KEYS, ROWS), F32),
            vm((8, KEYS, ROWS), F32),
            vm((8, 2, 8, ROWS), F32),
            vm((8, 4, 128), F32),
            vm((8, 4, 128), F32),
            vm((8, 4, 128), F32),
            vm((KEYS, WIDTH), F32),
            vm((KEYS, WIDTH), F32),
            vm((WIDTH, ROWS), F32),
            vm((8, WIDTH, ROWS), BF16),
            vm((8, WIDTH, ROWS), BF16),
            vm((2, 2, ROWS, WIDTH), BF16),
            vm((2, 2, ROWS, WIDTH), BF16),
            vm((2, ROWS, WIDTH), BF16),
            vm((2, ROWS, WIDTH), BF16),
            vm((3, ROWS, WIDTH), F32),
            dma((4,)),
            dma((16,)),
            dma((16,)),
            dma((6,)),
            dma((6,)),
            dma((8,)),
            dma((8,)),
            dma((8,)),
            dma((8,)),
            dma((8,)),
            dma((8,)),
            dma((3,)),
            dma((3,)),
            dma((3,)),
        ],
        compiler_params=pltpu.CompilerParams(
            collective_id=0, has_side_effects=True, vmem_limit_bytes=56 * 1024 * 1024
        ),
        cost_estimate=pl.CostEstimate(
            flops=2 * 5 * KEYS * 8 * ROWS * WIDTH,
            bytes_accessed=4 * ROWS * WIDTH * 2 + 3 * ROWS * WIDTH * 4,
            transcendentals=KEYS * 8 * ROWS,
        ),
    )(queries, key_rows, value_rows, out_grad)


def solution(mesh):
    spec = P(("dp", "ctx"), None)
    return jax.shard_map(
        shards, mesh=mesh, in_specs=(spec,) * 4, out_specs=(spec,) * 3, check_vma=False
    )
```

```python
import math

import jax
import jax.numpy as jnp
from jax import lax
from jax.experimental import pallas as pl
from jax.experimental.pallas import tpu as pltpu
from jax.sharding import PartitionSpec as P

F32 = jnp.float32
BF16 = jnp.bfloat16
MESH = pl.DeviceIdType.MESH

ROWS = 256
WIDTH = 128
RING = 8
HALF = 512
KEYS = 1024
SCALE = WIDTH ** (-0.5)
EXP2_SCALE = SCALE * math.log2(math.e)

OWN, R1, L1, R2, L2, R3, L3, FAR = range(8)
PLACE = (0, -1, 1, -2, 2, -3, 3, 4)
SLOT_AT = {p % RING: s for s, p in enumerate(PLACE)}
MIRROR = tuple(SLOT_AT[-p % RING] for p in PLACE)
PIECE = 128


def rows_dot(left, right):
    return lax.dot_general(left, right, (((1,), (1,)), ((), ())), preferred_element_type=F32)


def kernel(
    q_hbm, k_hbm, v_hbm, g_hbm,
    dq_hbm, dk_hbm, dv_hbm,
    qbuf, gbuf, kbuf, vbuf, ktbuf, ebuf, dbuf, mbuf,
    part_tx, part_rx, dk_acc, dv_acc,
    dqt, dq_tx, dq_rx, pair_tx, pair_rx, far_tx, far_rx, out_buf,
    in_sem, gat_send, gat_recv, kv_send, kv_recv, st_send, st_recv,
    dq_send, dq_recv, red_send, red_recv, out_sem,
):
    me = lax.axis_index("ctx")
    z = me // 4
    w = me % 4
    core = w % 2
    xh = w // 2

    def on_ring(offset):
        return {"ctx": ((z + (offset + RING)) % RING) * 4 + w}

    sibling = {"ctx": z * 4 + xh * 2 + (1 - core)}
    across = {"ctx": z * 4 + (1 - xh) * 2 + core}
    right, left = on_ring(1), on_ring(-1)

    barrier = pltpu.get_barrier_semaphore()
    for peer in (right, left, across, sibling):
        pl.semaphore_signal(barrier, inc=1, device_id=peer, device_id_type=MESH)

    own_rows = pl.ds(0, ROWS)
    loads = [
        pltpu.make_async_copy(src, dst, in_sem.at[i])
        for i, (src, dst) in enumerate(
            (
                (q_hbm, qbuf.at[OWN]),
                (g_hbm, gbuf.at[OWN]),
                (k_hbm, kbuf.at[own_rows]),
                (v_hbm, vbuf.at[own_rows]),
            )
        )
    ]
    for c in loads:
        c.start()
    pending = []

    def send(src, dst, send_sem, recv_sem, peer):
        c = pltpu.make_async_remote_copy(
            src_ref=src, dst_ref=dst, send_sem=send_sem, recv_sem=recv_sem,
            device_id=peer, device_id_type=MESH,
        )
        c.start()
        pending.append(c)
        return c

    for c in loads:
        c.wait()
    pl.semaphore_wait(barrier, 4)

    def hop(b, d, i):
        slots = ((OWN, R1, R2, R3, FAR), (OWN, L1, L2, L3, FAR))[d]
        n = (b * 2 + d) * 4 + i
        buf = (qbuf, gbuf)[b // 2]
        rows = pl.ds((b % 2) * PIECE, PIECE)
        return send(
            buf.at[slots[i], rows], buf.at[slots[i + 1], rows],
            gat_send.at[n], gat_recv.at[n], (right, left)[d],
        )

    def key_rows_at(p):
        return pl.ds(p * ROWS, ROWS)

    hops = {}
    for b in range(4):
        for d in (0, 1):
            hops[b, d, 0] = hop(b, d, 0)
    kv_across = []
    for i, buf in enumerate((kbuf, vbuf)):
        kv_across.append(
            send(buf.at[key_rows_at(0)], buf.at[key_rows_at(2)], kv_send.at[i], kv_recv.at[i], across)
        )
    kv_sibling = []
    for i, buf in enumerate((kbuf, vbuf)):
        kv_sibling.append(
            send(buf.at[key_rows_at(0)], buf.at[key_rows_at(1)], kv_send.at[2 + i], kv_recv.at[2 + i], sibling)
        )
    kv_third = []

    def pass_keys_on():
        for i, buf in enumerate((kbuf, vbuf)):
            kv_across[i].wait_recv()
            kv_third.append(
                send(buf.at[key_rows_at(2)], buf.at[key_rows_at(3)], kv_send.at[4 + i], kv_recv.at[4 + i], sibling)
            )

    def tile(slot, kh):
        keys = pl.ds(kh * HALF, HALF)
        s = rows_dot(kbuf[keys, :], qbuf[slot])
        m = jnp.max(s, axis=0, keepdims=True)
        e = jnp.exp2((s - m) * EXP2_SCALE)
        ebuf[slot, keys, :] = e
        d = rows_dot(vbuf[keys, :], gbuf[slot])
        dbuf[slot, keys, :] = d
        mbuf[slot, kh, 0:1, :] = m * SCALE
        mbuf[slot, kh, 1:2, :] = jnp.sum(e, axis=0, keepdims=True)
        mbuf[slot, kh, 2:3, :] = jnp.sum(e * d, axis=0, keepdims=True)

    def stats(slot):
        m0, l0, w0 = (mbuf[slot, 0, i : i + 1, :] for i in range(3))
        m1, l1, w1 = (mbuf[slot, 1, i : i + 1, :] for i in range(3))
        m = jnp.maximum(m0, m1)
        a0, a1 = jnp.exp(m0 - m), jnp.exp(m1 - m)
        total = l0 * a0 + l1 * a1
        log_total = m + jnp.log(total)
        delta = (w0 * a0 + w1 * a1) / total
        for i in range(2):
            cols = slice(i * 128, (i + 1) * 128)
            part_tx[slot, i : i + 1, :] = log_total[:, cols]
            part_tx[slot, 2 + i : 3 + i, :] = delta[:, cols]

    groups = (pl.ds(0, 5), pl.ds(5, 2), pl.ds(7, 1))
    st = {}

    def share_stats(g):
        for slot in (FAR, R3, L3, R2, L2, R1, L1):
            at = MIRROR[slot]
            st[at, g] = send(
                part_tx.at[groups[g]], part_rx.at[at, groups[g]],
                st_send.at[slot, g], st_recv.at[at, g], on_ring(PLACE[slot]),
            )

    def arrive(b, i):
        for d in (0, 1):
            hops[b, d, i].wait_recv()
            if i < 2 or b // 2 == d:
                hops[b, d, i + 1] = hop(b, d, i + 1)

    for c in kv_sibling:
        c.wait_recv()
    tile(OWN, 0)
    for b in range(4):
        arrive(b, 0)
    tile(R1, 0)
    pass_keys_on()
    tile(L1, 0)
    arrive(0, 1)
    for c in kv_third:
        c.wait_recv()
    tile(OWN, 1)
    arrive(1, 1)
    tile(R1, 1)
    arrive(2, 1)
    tile(L1, 1)
    arrive(3, 1)
    for slot in (OWN, R1, L1):
        stats(slot)
    tile(R2, 0)
    tile(R2, 1)
    arrive(0, 2)
    arrive(1, 2)
    tile(L2, 0)
    arrive(2, 2)
    tile(L2, 1)
    arrive(3, 2)
    stats(R2)
    stats(L2)
    share_stats(0)
    for slot in (R3, L3):
        tile(slot, 0)
        tile(slot, 1)
        stats(slot)
    share_stats(1)
    for p in range(4):
        ktbuf[:, p * ROWS : (p + 1) * ROWS] = kbuf[key_rows_at(p), :].astype(F32).T.astype(BF16)
    for b in range(4):
        hops[b, b // 2, 3].wait_recv()
    tile(FAR, 0)
    tile(FAR, 1)
    stats(FAR)
    share_stats(2)

    order = (FAR, R3, L3, R2, L2, R1, L1, OWN)
    for g in range(2):
        for u in range(1, 8):
            st[u, g].wait_recv()
    partial = {}

    def parts_of(t, u):
        s = SLOT_AT[(PLACE[t] - PLACE[u]) % RING]
        ref = part_tx if u == OWN else part_rx.at[u]
        return s, ref

    def combine(parts):
        peak = parts[0][0]
        for part in parts[1:]:
            peak = jnp.maximum(peak, part[0])
        total = jnp.zeros_like(peak)
        weighted = jnp.zeros_like(peak)
        for log_part, delta_part in parts:
            share = jnp.exp(log_part - peak)
            total = total + share
            weighted = weighted + share * delta_part
        return peak + jnp.log(total), weighted / total

    for t in order:
        early = []
        for u in range(8):
            s, ref = parts_of(t, u)
            if s != FAR:
                early.append((ref[s, 0:2, :], ref[s, 2:4, :]))
        partial[t] = combine(early)
    for u in range(1, 8):
        st[u, 2].wait_recv()

    first = [True]

    def grads(slot):
        u = SLOT_AT[(PLACE[slot] - 4) % RING]
        s, ref = parts_of(slot, u)
        log_total, delta = combine([partial[slot], (ref[s, 0:2, :], ref[s, 2:4, :])])
        log_total = jnp.concatenate([log_total[0:1], log_total[1:2]], axis=1)
        delta = jnp.concatenate([delta[0:1], delta[1:2]], axis=1)
        dq_t = None
        for kh in range(2):
            keys = pl.ds(kh * HALF, HALF)
            c = jnp.exp(mbuf[slot, kh, 0:1, :] - log_total)
            p = ebuf[slot, keys, :] * c
            prob_half = p.astype(BF16)
            score_grad = (p * (dbuf[slot, keys, :] - delta)).astype(BF16)
            dv = jnp.dot(prob_half, gbuf[slot], preferred_element_type=F32)
            dk = jnp.dot(score_grad, qbuf[slot], preferred_element_type=F32)
            if first[0]:
                dv_acc[keys, :] = dv
                dk_acc[keys, :] = dk
            else:
                dv_acc[keys, :] += dv
                dk_acc[keys, :] += dk
            t = jnp.dot(ktbuf[:, keys], score_grad, preferred_element_type=F32)
            dq_t = t if dq_t is None else dq_t + t
        first[0] = False
        return dq_t

    dq = {}
    whole = pl.ds(0, WIDTH)
    far_rows = (pl.ds(0, 64), pl.ds(64, 64))

    def send_sum(d, kind, value):
        n = d * 4 + kind
        rows = far_rows[d] if kind == 0 else whole
        dq_tx[n, rows, :] = value.astype(BF16)
        steps = (2, 1, 2, 1)[kind]
        dq[d, kind] = send(
            dq_tx.at[n, rows], dq_rx.at[n, rows], dq_send.at[n], dq_recv.at[n],
            on_ring(steps if d else -steps),
        )

    t = grads(FAR)
    send_sum(0, 0, t[0:64])
    send_sum(1, 0, t[64:128])
    send_sum(0, 1, grads(R3))
    send_sum(1, 1, grads(L3))
    dqt[0] = grads(R2)
    dqt[1] = grads(L2)
    send_sum(0, 3, grads(R1))
    send_sum(1, 3, grads(L1))
    dqt[2] = grads(OWN)

    red = []
    for j, p in enumerate((3, 1)):
        pair_tx[j, 0] = dk_acc[key_rows_at(p), :].astype(BF16)
        pair_tx[j, 1] = dv_acc[key_rows_at(p), :].astype(BF16)
        red.append(send(pair_tx.at[j], pair_rx.at[j], red_send.at[j], red_recv.at[j], sibling))
    for d in (0, 1):
        dq[d, 0].wait_recv()
        dq[d, 1].wait_recv()
        dqt[d, far_rows[d], :] += dq_rx[d * 4, far_rows[d], :].astype(F32)
        send_sum(d, 2, dqt[d] + dq_rx[d * 4 + 1].astype(F32))
    red[0].wait_recv()
    far_tx[0] = (dk_acc[key_rows_at(2), :] + pair_rx[0, 0].astype(F32)).astype(BF16)
    far_tx[1] = (dv_acc[key_rows_at(2), :] + pair_rx[0, 1].astype(F32)).astype(BF16)
    red.append(send(far_tx, far_rx, red_send.at[2], red_recv.at[2], across))

    for d in (0, 1):
        dq[d, 3].wait_recv()
    t = dqt[2] + dq_rx[3].astype(F32) + dq_rx[7].astype(F32)
    for d in (0, 1):
        dq[d, 2].wait_recv()
    t = t + dq_rx[2].astype(F32) + dq_rx[6].astype(F32)
    out_buf[0] = t.T * SCALE
    outs = [pltpu.make_async_copy(out_buf.at[0], dq_hbm, out_sem.at[0])]
    outs[0].start()
    red[1].wait_recv()
    red[2].wait_recv()
    for i, (acc, out, scale) in enumerate(((dk_acc, dk_hbm, SCALE), (dv_acc, dv_hbm, None))):
        t = acc[key_rows_at(0), :] + pair_rx[1, i].astype(F32) + far_rx[i].astype(F32)
        out_buf[1 + i] = t if scale is None else t * scale
        c = pltpu.make_async_copy(out_buf.at[1 + i], out, out_sem.at[1 + i])
        c.start()
        outs.append(c)
    for c in pending:
        c.wait_send()
    for c in outs:
        c.wait()


def shards(queries, key_rows, value_rows, out_grad):
    any_spec = pl.BlockSpec(memory_space=pl.ANY)
    dma = pltpu.SemaphoreType.DMA
    out = jax.ShapeDtypeStruct((ROWS, WIDTH), F32)
    vm = pltpu.VMEM
    return pl.pallas_call(
        kernel,
        out_shape=(out, out, out),
        in_specs=[any_spec] * 4,
        out_specs=(any_spec,) * 3,
        scratch_shapes=[
            vm((8, ROWS, WIDTH), BF16),
            vm((8, ROWS, WIDTH), BF16),
            vm((KEYS, WIDTH), BF16),
            vm((KEYS, WIDTH), BF16),
            vm((WIDTH, KEYS), BF16),
            vm((8, KEYS, ROWS), F32),
            vm((8, KEYS, ROWS), F32),
            vm((8, 2, 8, ROWS), F32),
            vm((8, 4, 128), F32),
            vm((8, 8, 4, 128), F32),
            vm((KEYS, WIDTH), F32),
            vm((KEYS, WIDTH), F32),
            vm((3, WIDTH, ROWS), F32),
            vm((8, WIDTH, ROWS), BF16),
            vm((8, WIDTH, ROWS), BF16),
            vm((2, 2, ROWS, WIDTH), BF16),
            vm((2, 2, ROWS, WIDTH), BF16),
            vm((2, ROWS, WIDTH), BF16),
            vm((2, ROWS, WIDTH), BF16),
            vm((3, ROWS, WIDTH), F32),
            dma((4,)),
            dma((32,)),
            dma((32,)),
            dma((6,)),
            dma((6,)),
            dma((8, 3)),
            dma((8, 3)),
            dma((8,)),
            dma((8,)),
            dma((3,)),
            dma((3,)),
            dma((3,)),
        ],
        compiler_params=pltpu.CompilerParams(
            collective_id=0, has_side_effects=True, vmem_limit_bytes=56 * 1024 * 1024
        ),
        cost_estimate=pl.CostEstimate(
            flops=2 * 5 * KEYS * 8 * ROWS * WIDTH,
            bytes_accessed=4 * ROWS * WIDTH * 2 + 3 * ROWS * WIDTH * 4,
            transcendentals=KEYS * 8 * ROWS,
        ),
    )(queries, key_rows, value_rows, out_grad)


def solution(mesh):
    spec = P(("dp", "ctx"), None)
    return jax.shard_map(
        shards, mesh=mesh, in_specs=(spec,) * 4, out_specs=(spec,) * 3, check_vma=False
    )
```

```python
import math

import jax
import jax.numpy as jnp
from jax import lax
from jax.experimental import pallas as pl
from jax.experimental.pallas import tpu as pltpu
from jax.sharding import PartitionSpec as P

F32 = jnp.float32
BF16 = jnp.bfloat16
MESH = pl.DeviceIdType.MESH

ROWS = 256
WIDTH = 128
RING = 8
HALF = 512
KEYS = 1024
SCALE = WIDTH ** (-0.5)
EXP2_SCALE = SCALE * math.log2(math.e)

OWN, R1, L1, R2, L2, R3, L3, FAR = range(8)
PLACE = (0, -1, 1, -2, 2, -3, 3, 4)
SLOT_AT = {p % RING: s for s, p in enumerate(PLACE)}
MIRROR = tuple(SLOT_AT[-p % RING] for p in PLACE)
PIECE = 128

Q_PATH = ((OWN, R1, 1), (OWN, L1, -1), (R1, R2, 1), (L1, L2, -1), (R2, FAR, 2), (R2, R3, 1), (L2, L3, -1))
G_PATH = ((OWN, R1, 1), (OWN, L1, -1), (R1, R2, 1), (L1, L2, -1), (L2, FAR, -2), (R2, R3, 1), (L2, L3, -1))
PIECES = ((0, 2), (1, 3), (2, 0), (3, 1))


def rows_dot(left, right):
    return lax.dot_general(left, right, (((1,), (1,)), ((), ())), preferred_element_type=F32)


def kernel(
    q_hbm, k_hbm, v_hbm, g_hbm,
    dq_out, dk_out, dv_out,
    qbuf, gbuf, kbuf, vbuf, ktbuf, ebuf, dbuf, mbuf,
    part_tx, part_rx, dk_acc, dv_acc,
    dqt, dq_tx, dq_rx, pair_tx, pair_rx, far_tx, far_rx,
    in_sem, gat_send, gat_recv, kv_send, kv_recv, st_send, st_recv,
    dq_send, dq_recv, red_send, red_recv,
):
    me = lax.axis_index("ctx")
    z = me // 4
    w = me % 4
    core = w % 2
    xh = w // 2

    def on_ring(offset):
        return {"ctx": ((z + (offset + RING)) % RING) * 4 + w}

    sibling = {"ctx": z * 4 + xh * 2 + (1 - core)}
    across = {"ctx": z * 4 + (1 - xh) * 2 + core}
    right, left = on_ring(1), on_ring(-1)

    barrier = pltpu.get_barrier_semaphore()
    for peer in (right, left, across, sibling):
        pl.semaphore_signal(barrier, inc=1, device_id=peer, device_id_type=MESH)

    own_rows = pl.ds(0, ROWS)
    loads = [
        pltpu.make_async_copy(src, dst, in_sem.at[i])
        for i, (src, dst) in enumerate(
            (
                (q_hbm, qbuf.at[OWN]),
                (g_hbm, gbuf.at[OWN]),
                (k_hbm, kbuf.at[own_rows]),
                (v_hbm, vbuf.at[own_rows]),
            )
        )
    ]
    for c in loads:
        c.start()
    pending = []

    def send(src, dst, send_sem, recv_sem, peer):
        c = pltpu.make_async_remote_copy(
            src_ref=src, dst_ref=dst, send_sem=send_sem, recv_sem=recv_sem,
            device_id=peer, device_id_type=MESH,
        )
        c.start()
        pending.append(c)
        return c

    for c in loads:
        c.wait()
    pl.semaphore_wait(barrier, 4)

    hops = {}

    def pass_on(piece, slot, way=None):
        buf, path = ((qbuf, Q_PATH), (gbuf, G_PATH))[piece // 2]
        rows = pl.ds((piece % 2) * PIECE, PIECE)
        for src, dst, steps in path:
            if src == slot and way in (None, steps > 0):
                n = piece * 8 + dst
                hops[piece, dst] = send(
                    buf.at[src, rows], buf.at[dst, rows], gat_send.at[n], gat_recv.at[n], on_ring(steps)
                )

    def arrive(piece, slot):
        hops[piece, slot].wait_recv()
        pass_on(piece, slot)

    def key_rows_at(p):
        return pl.ds(p * ROWS, ROWS)

    for a, b in PIECES:
        pass_on(a, OWN, True)
        pass_on(b, OWN, False)
    kv_across = []
    for i, buf in enumerate((kbuf, vbuf)):
        kv_across.append(
            send(buf.at[key_rows_at(0)], buf.at[key_rows_at(2)], kv_send.at[i], kv_recv.at[i], across)
        )
    kv_sibling = []
    for i, buf in enumerate((kbuf, vbuf)):
        kv_sibling.append(
            send(buf.at[key_rows_at(0)], buf.at[key_rows_at(1)], kv_send.at[2 + i], kv_recv.at[2 + i], sibling)
        )
    kv_third = []

    def pass_keys_on():
        for i, buf in enumerate((kbuf, vbuf)):
            kv_across[i].wait_recv()
            kv_third.append(
                send(buf.at[key_rows_at(2)], buf.at[key_rows_at(3)], kv_send.at[4 + i], kv_recv.at[4 + i], sibling)
            )

    def tile(slot, kh):
        keys = pl.ds(kh * HALF, HALF)
        s = rows_dot(kbuf[keys, :], qbuf[slot])
        m = jnp.max(s, axis=0, keepdims=True)
        e = jnp.exp2((s - m) * EXP2_SCALE)
        ebuf[slot, keys, :] = e
        d = rows_dot(vbuf[keys, :], gbuf[slot])
        dbuf[slot, keys, :] = d
        mbuf[slot, kh, 0:1, :] = m * SCALE
        mbuf[slot, kh, 1:2, :] = jnp.sum(e, axis=0, keepdims=True)
        mbuf[slot, kh, 2:3, :] = jnp.sum(e * d, axis=0, keepdims=True)

    def stats(slot):
        m0, l0, w0 = (mbuf[slot, 0, i : i + 1, :] for i in range(3))
        m1, l1, w1 = (mbuf[slot, 1, i : i + 1, :] for i in range(3))
        m = jnp.maximum(m0, m1)
        a0, a1 = jnp.exp(m0 - m), jnp.exp(m1 - m)
        total = l0 * a0 + l1 * a1
        log_total = m + jnp.log(total)
        delta = (w0 * a0 + w1 * a1) / total
        for i in range(2):
            cols = slice(i * 128, (i + 1) * 128)
            part_tx[slot, i : i + 1, :] = log_total[:, cols]
            part_tx[slot, 2 + i : 3 + i, :] = delta[:, cols]

    groups = (pl.ds(0, 5), pl.ds(5, 2), pl.ds(7, 1))
    st = {}

    def share_stats(g):
        for slot in (FAR, R3, L3, R2, L2, R1, L1):
            at = MIRROR[slot]
            st[at, g] = send(
                part_tx.at[groups[g]], part_rx.at[at, groups[g]],
                st_send.at[slot, g], st_recv.at[at, g], on_ring(PLACE[slot]),
            )

    for c in kv_sibling:
        c.wait_recv()
    tile(OWN, 0)
    for a, b in PIECES:
        arrive(a, R1)
        arrive(b, L1)
    pass_keys_on()
    tile(R1, 0)
    tile(L1, 0)
    for a, b in PIECES[:2]:
        arrive(a, R2)
        arrive(b, L2)
    for c in kv_third:
        c.wait_recv()
    tile(OWN, 1)
    for a, b in PIECES[2:]:
        arrive(a, R2)
        arrive(b, L2)
    for slot in (R1, L1):
        tile(slot, 1)
    for slot in (OWN, R1, L1):
        stats(slot)
    for slot in (R2, L2):
        tile(slot, 0)
        tile(slot, 1)
        stats(slot)
    for p in range(4):
        ktbuf[:, p * ROWS : (p + 1) * ROWS] = kbuf[key_rows_at(p), :].astype(F32).T.astype(BF16)
    for slot in (R3, L3):
        for piece in range(4):
            arrive(piece, slot)
        if slot == R3:
            share_stats(0)
        tile(slot, 0)
        tile(slot, 1)
        stats(slot)
    share_stats(1)
    for piece in range(4):
        arrive(piece, FAR)
    tile(FAR, 0)
    tile(FAR, 1)
    stats(FAR)
    share_stats(2)

    order = (FAR, R3, L3, R2, L2, R1, L1, OWN)
    for g in range(2):
        for u in range(1, 8):
            st[u, g].wait_recv()
    partial = {}

    def parts_of(t, u):
        s = SLOT_AT[(PLACE[t] - PLACE[u]) % RING]
        ref = part_tx if u == OWN else part_rx.at[u]
        return s, ref

    def combine(parts):
        peak = parts[0][0]
        for part in parts[1:]:
            peak = jnp.maximum(peak, part[0])
        total = jnp.zeros_like(peak)
        weighted = jnp.zeros_like(peak)
        for log_part, delta_part in parts:
            share = jnp.exp(log_part - peak)
            total = total + share
            weighted = weighted + share * delta_part
        return peak + jnp.log(total), weighted / total

    for t in order:
        early = []
        for u in range(8):
            s, ref = parts_of(t, u)
            if s != FAR:
                early.append((ref[s, 0:2, :], ref[s, 2:4, :]))
        partial[t] = combine(early)
    for u in range(1, 8):
        st[u, 2].wait_recv()

    rows_stats = {}

    def grads(slot, kh):
        if slot not in rows_stats:
            u = SLOT_AT[(PLACE[slot] - 4) % RING]
            s, ref = parts_of(slot, u)
            log_total, delta = combine([partial[slot], (ref[s, 0:2, :], ref[s, 2:4, :])])
            rows_stats[slot] = tuple(
                jnp.concatenate([x[0:1], x[1:2]], axis=1) for x in (log_total, delta)
            )
        log_total, delta = rows_stats[slot]
        keys = pl.ds(kh * HALF, HALF)
        c = jnp.exp(mbuf[slot, kh, 0:1, :] - log_total)
        p = ebuf[slot, keys, :] * c
        prob_half = p.astype(BF16)
        score_grad = (p * (dbuf[slot, keys, :] - delta)).astype(BF16)
        dv = jnp.dot(prob_half, gbuf[slot], preferred_element_type=F32)
        dk = jnp.dot(score_grad, qbuf[slot], preferred_element_type=F32)
        if slot == R3:
            dv_acc[keys, :] = dv
            dk_acc[keys, :] = dk
        else:
            dv_acc[keys, :] += dv
            dk_acc[keys, :] += dk
        return jnp.dot(ktbuf[:, keys], score_grad, preferred_element_type=F32)

    dq = {}

    def send_sum(d, kind, h, value):
        n = (d * 4 + kind) * 2 + h
        dq_tx[n] = value.astype(BF16)
        steps = (4, 1, 2, 1)[kind]
        dq[d, kind, h] = send(
            dq_tx.at[n], dq_rx.at[n], dq_send.at[n], dq_recv.at[n], on_ring(steps if d else -steps)
        )

    def received(d, kind, h):
        dq[d, kind, h].wait_recv()
        return dq_rx[(d * 4 + kind) * 2 + h].astype(F32)

    wide = (slice(0, 64), slice(64, 128))
    for d, slot in enumerate((R3, L3)):
        t = grads(slot, 0) + grads(slot, 1)
        for h in (0, 1):
            send_sum(d, 1, h, t[wide[h]])
    t = grads(FAR, 0) + grads(FAR, 1)
    for h in (0, 1):
        send_sum(h, 0, h, t[wide[h]])
    for d, slot in enumerate((R2, L2)):
        dqt[slot] = grads(slot, 1) + grads(slot, 0)

    for slot in (R1, L1, OWN):
        dqt[slot] = grads(slot, 1)
    accs = (dk_acc, dv_acc)
    pair = {}
    across_sum = []

    def send_pair(j, p):
        for i, acc in enumerate(accs):
            n = j * 2 + i
            pair_tx[n] = acc[key_rows_at(p), :].astype(BF16)
            pair[j, i] = send(pair_tx.at[n], pair_rx.at[n], red_send.at[n], red_recv.at[n], sibling)

    def from_pair(j, i):
        pair[j, i].wait_recv()
        return pair_rx[j * 2 + i].astype(F32)

    send_pair(0, 3)
    for d, slot in enumerate((R1, L1)):
        t = dqt[slot] + grads(slot, 0)
        for h in (0, 1):
            send_sum(d, 3, h, t[wide[h]])
    dqt[OWN] += grads(OWN, 0)
    send_pair(1, 1)
    for i, acc in enumerate(accs):
        far_tx[i] = (acc[key_rows_at(2), :] + from_pair(0, i)).astype(BF16)
        across_sum.append(
            send(far_tx.at[i], far_rx.at[i], red_send.at[4 + i], red_recv.at[4 + i], across)
        )
    for d, slot in enumerate((R2, L2)):
        for h in (0, 1):
            send_sum(d, 2, h, dqt[slot, wide[h], :] + received(d, 1, h))

    for h in (0, 1):
        for d in (0, 1):
            dqt[OWN, wide[h], :] += received(d, 3, h)
    for h in (0, 1):
        dqt[OWN, wide[h], :] += received(h, 0, h)
    for i, (acc, out, scale) in enumerate(((dk_acc, dk_out, SCALE), (dv_acc, dv_out, None))):
        t = acc[key_rows_at(0), :] + from_pair(1, i)
        across_sum[i].wait_recv()
        t = t + far_rx[i].astype(F32)
        out[...] = t if scale is None else t * scale
    for h in (0, 1):
        for d in (0, 1):
            dqt[OWN, wide[h], :] += received(d, 2, h)
    dq_out[...] = dqt[OWN].T * SCALE
    for c in pending:
        c.wait_send()


def write_out(a_ref, b_ref, c_ref, a_out, b_out, c_out, sems):
    copies = [
        pltpu.make_async_copy(src, dst, sems.at[i])
        for i, (src, dst) in enumerate(((a_ref, a_out), (b_ref, b_out), (c_ref, c_out)))
    ]
    for c in copies:
        c.start()
    for c in copies:
        c.wait()


def shards(queries, key_rows, value_rows, out_grad):
    any_spec = pl.BlockSpec(memory_space=pl.ANY)
    dma = pltpu.SemaphoreType.DMA
    out = jax.ShapeDtypeStruct((ROWS, WIDTH), F32)
    near = pltpu.VMEM((ROWS, WIDTH), F32)
    near_spec = pl.BlockSpec(memory_space=pltpu.VMEM)
    vm = pltpu.VMEM
    grads = pl.pallas_call(
        kernel,
        out_shape=(near, near, near),
        in_specs=[any_spec] * 4,
        out_specs=(near_spec,) * 3,
        scratch_shapes=[
            vm((8, ROWS, WIDTH), BF16),
            vm((8, ROWS, WIDTH), BF16),
            vm((KEYS, WIDTH), BF16),
            vm((KEYS, WIDTH), BF16),
            vm((WIDTH, KEYS), BF16),
            vm((8, KEYS, ROWS), F32),
            vm((8, KEYS, ROWS), F32),
            vm((8, 2, 8, ROWS), F32),
            vm((8, 4, 128), F32),
            vm((8, 8, 4, 128), F32),
            vm((KEYS, WIDTH), F32),
            vm((KEYS, WIDTH), F32),
            vm((5, WIDTH, ROWS), F32),
            vm((16, WIDTH // 2, ROWS), BF16),
            vm((16, WIDTH // 2, ROWS), BF16),
            vm((4, ROWS, WIDTH), BF16),
            vm((4, ROWS, WIDTH), BF16),
            vm((2, ROWS, WIDTH), BF16),
            vm((2, ROWS, WIDTH), BF16),
            dma((4,)),
            dma((32,)),
            dma((32,)),
            dma((6,)),
            dma((6,)),
            dma((8, 3)),
            dma((8, 3)),
            dma((16,)),
            dma((16,)),
            dma((6,)),
            dma((6,)),
        ],
        compiler_params=pltpu.CompilerParams(
            collective_id=0, has_side_effects=True, vmem_limit_bytes=56 * 1024 * 1024
        ),
        cost_estimate=pl.CostEstimate(
            flops=2 * 5 * KEYS * 8 * ROWS * WIDTH,
            bytes_accessed=4 * ROWS * WIDTH * 2 + 3 * ROWS * WIDTH * 4,
            transcendentals=KEYS * 8 * ROWS,
        ),
    )(queries, key_rows, value_rows, out_grad)
    return pl.pallas_call(
        write_out,
        out_shape=(out, out, out),
        in_specs=[near_spec] * 3,
        out_specs=(any_spec,) * 3,
        scratch_shapes=[dma((3,))],
        compiler_params=pltpu.CompilerParams(vmem_limit_bytes=1024*1024),
    )(*grads)


def solution(mesh):
    spec = P(("dp", "ctx"), None)
    return jax.shard_map(
        shards, mesh=mesh, in_specs=(spec,) * 4, out_specs=(spec,) * 3, check_vma=False
    )
```

```python
import math

import jax
import jax.numpy as jnp
from jax import lax
from jax.experimental import pallas as pl
from jax.experimental.pallas import tpu as pltpu
from jax.sharding import PartitionSpec as P

F32 = jnp.float32
BF16 = jnp.bfloat16
MESH = pl.DeviceIdType.MESH

ROWS = 256
WIDTH = 128
RING = 8
HALF = 512
KEYS = 1024
SCALE = WIDTH ** (-0.5)
EXP2_SCALE = SCALE * math.log2(math.e)

R1, L1, R2, L2, R3, L3, OWN, FAR = range(8)
PLACE = (-1, 1, -2, 2, -3, 3, 0, 4)
SLOT_AT = {p % RING: s for s, p in enumerate(PLACE)}
MIRROR = tuple(SLOT_AT[-p % RING] for p in PLACE)
PEERS = (FAR, R3, L3, R2, L2, R1, L1)
PART = 128

Q_PATH = ((OWN, R1, 1), (OWN, L1, -1), (R1, R2, 1), (L1, L2, -1), (R2, FAR, 2), (R2, R3, 1), (L2, L3, -1))
G_PATH = ((OWN, R1, 1), (OWN, L1, -1), (R1, R2, 1), (L1, L2, -1), (L2, FAR, -2), (R2, R3, 1), (L2, L3, -1))
PIECES = ((0, 2), (2, 0), (1, 3), (3, 1))


def rows_dot(left, right):
    return lax.dot_general(left, right, (((1,), (1,)), ((), ())), preferred_element_type=F32)


def kernel(
    q_hbm, k_hbm, v_hbm, g_hbm,
    dq_out, dk_out, dv_out,
    qbuf, gbuf, kbuf, vbuf, ktbuf, ebuf, dbuf, mbuf,
    part_tx, part_rx, dk_acc, dv_acc,
    dqt, dq_tx, dq_rx, pair_tx, pair_rx, far_tx, far_rx,
    in_sem, gat_send, gat_recv, kv_send, kv_recv, st_send, st_recv,
    dq_send, dq_recv, red_send, red_recv,
):
    me = lax.axis_index("ctx")
    z = me // 4
    w = me % 4
    core = w % 2
    xh = w // 2

    def on_ring(offset):
        return {"ctx": ((z + (offset + RING)) % RING) * 4 + w}

    sibling = {"ctx": z * 4 + xh * 2 + (1 - core)}
    across = {"ctx": z * 4 + (1 - xh) * 2 + core}
    right, left = on_ring(1), on_ring(-1)

    barrier = pltpu.get_barrier_semaphore()
    for peer in (right, left, across, sibling):
        pl.semaphore_signal(barrier, inc=1, device_id=peer, device_id_type=MESH)

    own_rows = pl.ds(0, ROWS)
    loads = [
        pltpu.make_async_copy(src, dst, in_sem.at[i])
        for i, (src, dst) in enumerate(
            (
                (q_hbm.at[pl.ds(0, PART)], qbuf.at[0, OWN]),
                (g_hbm.at[pl.ds(0, PART)], gbuf.at[0, OWN]),
                (q_hbm.at[pl.ds(PART, PART)], qbuf.at[1, OWN]),
                (g_hbm.at[pl.ds(PART, PART)], gbuf.at[1, OWN]),
                (k_hbm, kbuf.at[own_rows]),
                (v_hbm, vbuf.at[own_rows]),
            )
        )
    ]
    for c in loads:
        c.start()
    pending = []

    def send(src, dst, send_sem, recv_sem, peer):
        c = pltpu.make_async_remote_copy(
            src_ref=src, dst_ref=dst, send_sem=send_sem, recv_sem=recv_sem,
            device_id=peer, device_id_type=MESH,
        )
        c.start()
        pending.append(c)
        return c

    for c in loads:
        c.wait()
    pl.semaphore_wait(barrier, 4)

    hops = {}

    def pass_on(piece, slot, way=None):
        buf, path = ((qbuf, Q_PATH), (gbuf, G_PATH))[piece // 2]
        half = piece % 2
        for src, dst, steps in path:
            if src == slot and way in (None, steps > 0):
                n = piece * 8 + dst
                hops[piece, dst] = send(
                    buf.at[half, src], buf.at[half, dst], gat_send.at[n], gat_recv.at[n], on_ring(steps)
                )

    def arrive(piece, slot):
        hops[piece, slot].wait_recv()
        pass_on(piece, slot)

    def key_rows_at(p):
        return pl.ds(p * ROWS, ROWS)

    for a, b in PIECES:
        pass_on(a, OWN, True)
        pass_on(b, OWN, False)
    kv_across = []
    for i, buf in enumerate((kbuf, vbuf)):
        kv_across.append(
            send(buf.at[key_rows_at(0)], buf.at[key_rows_at(2)], kv_send.at[i], kv_recv.at[i], across)
        )
    kv_sibling = []
    for i, buf in enumerate((kbuf, vbuf)):
        kv_sibling.append(
            send(buf.at[key_rows_at(0)], buf.at[key_rows_at(1)], kv_send.at[2 + i], kv_recv.at[2 + i], sibling)
        )
    kv_third = []

    def pass_keys_on():
        for i, buf in enumerate((kbuf, vbuf)):
            kv_across[i].wait_recv()
            kv_third.append(
                send(buf.at[key_rows_at(2)], buf.at[key_rows_at(3)], kv_send.at[4 + i], kv_recv.at[4 + i], sibling)
            )

    def side_by_side(buf, half, pair):
        return buf[half, 2 * pair : 2 * pair + 2].reshape(2 * PART, WIDTH)

    def tile(half, pair):
        t = half * 4 + pair
        queries, grads_out = side_by_side(qbuf, half, pair), side_by_side(gbuf, half, pair)
        for kh in (0, 1):
            keys = pl.ds(kh * HALF, HALF)
            s = rows_dot(kbuf[keys, :], queries)
            m = jnp.max(s, axis=0, keepdims=True)
            e = jnp.exp2((s - m) * EXP2_SCALE)
            ebuf[t, keys, :] = e
            d = rows_dot(vbuf[keys, :], grads_out)
            dbuf[t, keys, :] = d
            mbuf[t, kh, 0:1, :] = m * SCALE
            mbuf[t, kh, 1:2, :] = jnp.sum(e, axis=0, keepdims=True)
            mbuf[t, kh, 2:3, :] = jnp.sum(e * d, axis=0, keepdims=True)
        m0, l0, w0 = (mbuf[t, 0, i : i + 1, :] for i in range(3))
        m1, l1, w1 = (mbuf[t, 1, i : i + 1, :] for i in range(3))
        m = jnp.maximum(m0, m1)
        a0, a1 = jnp.exp(m0 - m), jnp.exp(m1 - m)
        total = l0 * a0 + l1 * a1
        log_total = m + jnp.log(total)
        delta = (w0 * a0 + w1 * a1) / total
        for i in range(2):
            cols = slice(i * PART, (i + 1) * PART)
            part_tx[half, 2 * pair + i, 0:1, :] = log_total[:, cols]
            part_tx[half, 2 * pair + i, 1:2, :] = delta[:, cols]

    st = {}

    def share_stats(half, g):
        group = pl.ds(g * 4, 4)
        n = half * 2 + g
        for slot in PEERS:
            at = MIRROR[slot]
            st[at, half, g] = send(
                part_tx.at[half, group], part_rx.at[at, half, group],
                st_send.at[slot, n], st_recv.at[at, n], on_ring(PLACE[slot]),
            )

    def parts_of(half, t, g):
        found = []
        for u in range(8):
            s = SLOT_AT[(PLACE[t] - PLACE[u]) % RING]
            if s // 4 == g:
                ref = part_tx if u == OWN else part_rx.at[u]
                found.append((ref[half, s, 0:1, :], ref[half, s, 1:2, :]))
        return found

    def combine(parts):
        peak = parts[0][0]
        for part in parts[1:]:
            peak = jnp.maximum(peak, part[0])
        total = jnp.zeros_like(peak)
        weighted = jnp.zeros_like(peak)
        for log_part, delta_part in parts:
            share = jnp.exp(log_part - peak)
            total = total + share
            weighted = weighted + share * delta_part
        return peak + jnp.log(total), weighted / total

    partial = {}

    def early_stats(half):
        for slot in PEERS:
            st[slot, half, 0].wait_recv()
        for slot in range(8):
            partial[half, slot] = combine(parts_of(half, slot, 0))

    def late_stats(half):
        for slot in PEERS:
            st[slot, half, 1].wait_recv()

    rows_stats = {}

    def grads(half, pair, kh):
        t = half * 4 + pair
        if t not in rows_stats:
            both = [combine([partial[half, x]] + parts_of(half, x, 1)) for x in (2 * pair, 2 * pair + 1)]
            rows_stats[t] = tuple(jnp.concatenate(x, axis=1) for x in zip(*both))
        log_total, delta = rows_stats[t]
        keys = pl.ds(kh * HALF, HALF)
        c = jnp.exp(mbuf[t, kh, 0:1, :] - log_total)
        p = ebuf[t, keys, :] * c
        prob_half = p.astype(BF16)
        score_grad = (p * (dbuf[t, keys, :] - delta)).astype(BF16)
        dv = jnp.dot(prob_half, side_by_side(gbuf, half, pair), preferred_element_type=F32)
        dk = jnp.dot(score_grad, side_by_side(qbuf, half, pair), preferred_element_type=F32)
        if (half, pair) == (0, R3 // 2):
            dv_acc[keys, :] = dv
            dk_acc[keys, :] = dk
        else:
            dv_acc[keys, :] += dv
            dk_acc[keys, :] += dk
        return jnp.dot(ktbuf[:, keys], score_grad, preferred_element_type=F32)

    dq = {}
    sides = (slice(0, PART), slice(PART, 2 * PART))
    own_sum, far_sum = (0, 5), (1, 3)

    def send_sum(half, d, kind, value):
        n = (half * 2 + d) * 4 + kind
        dq_tx[n] = value.astype(BF16)
        steps = (4, 1, 2, 1)[kind]
        dq[half, d, kind] = send(
            dq_tx.at[n], dq_rx.at[n], dq_send.at[n], dq_recv.at[n], on_ring(steps if d else -steps)
        )

    def received(half, d, kind):
        dq[half, d, kind].wait_recv()
        return dq_rx[(half * 2 + d) * 4 + kind].astype(F32)

    def send_both(half, kind, value):
        for d in (0, 1):
            send_sum(half, d, kind, value[:, sides[d]])

    def far_sums(half):
        for d in (0, 1):
            send_sum(half, d, 2, dqt[far_sum[half], :, sides[d]] + received(half, d, 1))

    for a, b in PIECES:
        arrive(a, R1)
        arrive(b, L1)
    pass_keys_on()
    for a, b in PIECES[:2]:
        arrive(a, R2)
        arrive(b, L2)
    for c in kv_sibling + kv_third:
        c.wait_recv()
    tile(0, 0)
    for a, b in PIECES[2:]:
        arrive(a, R2)
        arrive(b, L2)
    tile(0, 1)
    tile(1, 0)
    for p in range(4):
        ktbuf[:, p * ROWS : (p + 1) * ROWS] = kbuf[key_rows_at(p), :].astype(F32).T.astype(BF16)
    for half in (0, 1):
        for piece in (half, 2 + half):
            arrive(piece, R3)
            arrive(piece, L3)
        share_stats(half, 0)
        tile(half, 2)
        for piece in (half, 2 + half):
            arrive(piece, FAR)
        tile(half, 3)
        share_stats(half, 1)
        if half == 0:
            tile(1, 1)

    early_stats(0)
    late_stats(0)
    send_both(0, 1, grads(0, 2, 0) + grads(0, 2, 1))
    t = grads(0, 3, 0) + grads(0, 3, 1)
    send_sum(0, 0, 0, t[:, sides[1]])
    dqt[0, :, sides[0]] = t[:, sides[0]]
    dqt[1] = grads(0, 1, 0) + grads(0, 1, 1)
    send_both(0, 3, grads(0, 0, 0) + grads(0, 0, 1))

    early_stats(1)
    late_stats(1)
    send_both(1, 1, grads(1, 2, 0) + grads(1, 2, 1))
    for pair in (3, 1, 0):
        dqt[2 + pair] = grads(1, pair, 1)
    accs = (dk_acc, dv_acc)
    pair_sum = {}
    across_sum = []

    def send_pair(j, p):
        for i, acc in enumerate(accs):
            n = j * 2 + i
            pair_tx[n] = acc[key_rows_at(p), :].astype(BF16)
            pair_sum[j, i] = send(pair_tx.at[n], pair_rx.at[n], red_send.at[n], red_recv.at[n], sibling)

    def from_pair(j, i):
        pair_sum[j, i].wait_recv()
        return pair_rx[j * 2 + i].astype(F32)

    send_pair(0, 3)
    t = dqt[5] + grads(1, 3, 0)
    send_sum(1, 0, 0, t[:, sides[1]])
    dqt[5, :, sides[0]] = t[:, sides[0]]
    far_sums(0)
    dqt[3] += grads(1, 1, 0)
    for i, acc in enumerate(accs):
        far_tx[i] = (acc[key_rows_at(2), :] + from_pair(0, i)).astype(BF16)
        across_sum.append(
            send(far_tx.at[i], far_rx.at[i], red_send.at[4 + i], red_recv.at[4 + i], across)
        )
    send_both(1, 3, dqt[2] + grads(1, 0, 0))
    send_pair(1, 1)
    far_sums(1)

    for half in (0, 1):
        t = dqt[own_sum[half], :, sides[0]] + received(half, 0, 0)
        for d in (0, 1):
            t = t + received(half, d, 3)
        if half == 0:
            for d in (0, 1):
                t = t + received(half, d, 2)
            dq_out[0:PART, :] = t.T * SCALE
        else:
            dqt[5, :, sides[0]] = t
    for i, (acc, out, scale) in enumerate(((dk_acc, dk_out, SCALE), (dv_acc, dv_out, None))):
        t = acc[key_rows_at(0), :] + from_pair(1, i)
        across_sum[i].wait_recv()
        t = t + far_rx[i].astype(F32)
        out[...] = t if scale is None else t * scale
    t = dqt[5, :, sides[0]]
    for d in (0, 1):
        t = t + received(1, d, 2)
    dq_out[PART : 2 * PART, :] = t.T * SCALE
    for c in pending:
        c.wait_send()


def write_out(a_ref, b_ref, c_ref, a_out, b_out, c_out, sems):
    copies = [
        pltpu.make_async_copy(src, dst, sems.at[i])
        for i, (src, dst) in enumerate(((a_ref, a_out), (b_ref, b_out), (c_ref, c_out)))
    ]
    for c in copies:
        c.start()
    for c in copies:
        c.wait()


def shards(queries, key_rows, value_rows, out_grad):
    any_spec = pl.BlockSpec(memory_space=pl.ANY)
    dma = pltpu.SemaphoreType.DMA
    out = jax.ShapeDtypeStruct((ROWS, WIDTH), F32)
    near = pltpu.VMEM((ROWS, WIDTH), F32)
    near_spec = pl.BlockSpec(memory_space=pltpu.VMEM)
    vm = pltpu.VMEM
    grads = pl.pallas_call(
        kernel,
        out_shape=(near, near, near),
        in_specs=[any_spec] * 4,
        out_specs=(near_spec,) * 3,
        scratch_shapes=[
            vm((2, 8, PART, WIDTH), BF16),
            vm((2, 8, PART, WIDTH), BF16),
            vm((KEYS, WIDTH), BF16),
            vm((KEYS, WIDTH), BF16),
            vm((WIDTH, KEYS), BF16),
            vm((8, KEYS, ROWS), F32),
            vm((8, KEYS, ROWS), F32),
            vm((8, 2, 8, ROWS), F32),
            vm((2, 8, 2, PART), F32),
            vm((8, 2, 8, 2, PART), F32),
            vm((KEYS, WIDTH), F32),
            vm((KEYS, WIDTH), F32),
            vm((6, WIDTH, 2 * PART), F32),
            vm((16, WIDTH, PART), BF16),
            vm((16, WIDTH, PART), BF16),
            vm((4, ROWS, WIDTH), BF16),
            vm((4, ROWS, WIDTH), BF16),
            vm((2, ROWS, WIDTH), BF16),
            vm((2, ROWS, WIDTH), BF16),
            dma((6,)),
            dma((32,)),
            dma((32,)),
            dma((6,)),
            dma((6,)),
            dma((8, 4)),
            dma((8, 4)),
            dma((16,)),
            dma((16,)),
            dma((6,)),
            dma((6,)),
        ],
        compiler_params=pltpu.CompilerParams(
            collective_id=0, has_side_effects=True, vmem_limit_bytes=56 * 1024 * 1024
        ),
        cost_estimate=pl.CostEstimate(
            flops=2 * 5 * KEYS * 8 * ROWS * WIDTH,
            bytes_accessed=4 * ROWS * WIDTH * 2 + 3 * ROWS * WIDTH * 4,
            transcendentals=KEYS * 8 * ROWS,
        ),
    )(queries, key_rows, value_rows, out_grad)
    return pl.pallas_call(
        write_out,
        out_shape=(out, out, out),
        in_specs=[near_spec] * 3,
        out_specs=(any_spec,) * 3,
        scratch_shapes=[dma((3,))],
        compiler_params=pltpu.CompilerParams(vmem_limit_bytes=1024*1024),
    )(*grads)


def solution(mesh):
    spec = P(("dp", "ctx"), None)
    return jax.shard_map(
        shards, mesh=mesh, in_specs=(spec,) * 4, out_specs=(spec,) * 3, check_vma=False
    )
```

```python
import math

import jax
import jax.numpy as jnp
from jax import lax
from jax.experimental import pallas as pl
from jax.experimental.pallas import tpu as pltpu
from jax.sharding import PartitionSpec as P

F32 = jnp.float32
BF16 = jnp.bfloat16
MESH = pl.DeviceIdType.MESH

ROWS = 256
WIDTH = 128
RING = 8
HALF = 512
KEYS = 1024
SCALE = WIDTH ** (-0.5)
EXP2_SCALE = SCALE * math.log2(math.e)

R1, L1, R2, L2, R3, L3, OWN, FAR = range(8)
PLACE = (-1, 1, -2, 2, -3, 3, 0, 4)
SLOT_AT = {p % RING: s for s, p in enumerate(PLACE)}
MIRROR = tuple(SLOT_AT[-p % RING] for p in PLACE)
PEERS = (FAR, R3, L3, R2, L2, R1, L1)
PART = 128

Q_PATH = ((OWN, R1, 1), (OWN, L1, -1), (R1, R2, 1), (L1, L2, -1), (R2, FAR, 2), (R2, R3, 1), (L2, L3, -1))
G_PATH = ((OWN, R1, 1), (OWN, L1, -1), (R1, R2, 1), (L1, L2, -1), (L2, FAR, -2), (R2, R3, 1), (L2, L3, -1))
PIECES = ((0, 2), (2, 0), (1, 3), (3, 1))


def rows_dot(left, right):
    return lax.dot_general(left, right, (((1,), (1,)), ((), ())), preferred_element_type=F32)


def kernel(
    q_hbm, k_hbm, v_hbm, g_hbm,
    dq_out, dk_out, dv_out,
    qbuf, gbuf, kbuf, vbuf, ktbuf, ebuf, dbuf, mbuf,
    part_tx, part_rx, dk_acc, dv_acc,
    dqt, dq_tx, dq_rx, pair_tx, pair_rx, far_tx, far_rx,
    in_sem, gat_send, gat_recv, kv_send, kv_recv, st_send, st_recv,
    dq_send, dq_recv, red_send, red_recv,
):
    me = lax.axis_index("ctx")
    z = me // 4
    w = me % 4
    core = w % 2
    xh = w // 2

    def on_ring(offset):
        return {"ctx": ((z + (offset + RING)) % RING) * 4 + w}

    sibling = {"ctx": z * 4 + xh * 2 + (1 - core)}
    across = {"ctx": z * 4 + (1 - xh) * 2 + core}
    right, left = on_ring(1), on_ring(-1)

    barrier = pltpu.get_barrier_semaphore()
    for peer in (right, left, across, sibling):
        pl.semaphore_signal(barrier, inc=1, device_id=peer, device_id_type=MESH)

    own_rows = pl.ds(0, ROWS)
    loads = [
        pltpu.make_async_copy(src, dst, in_sem.at[i])
        for i, (src, dst) in enumerate(
            (
                (q_hbm.at[pl.ds(0, PART)], qbuf.at[0, OWN]),
                (g_hbm.at[pl.ds(0, PART)], gbuf.at[0, OWN]),
                (q_hbm.at[pl.ds(PART, PART)], qbuf.at[1, OWN]),
                (g_hbm.at[pl.ds(PART, PART)], gbuf.at[1, OWN]),
                (k_hbm, kbuf.at[own_rows]),
                (v_hbm, vbuf.at[own_rows]),
            )
        )
    ]
    for c in loads:
        c.start()
    pending = []

    def send(src, dst, send_sem, recv_sem, peer):
        c = pltpu.make_async_remote_copy(
            src_ref=src, dst_ref=dst, send_sem=send_sem, recv_sem=recv_sem,
            device_id=peer, device_id_type=MESH,
        )
        c.start()
        pending.append(c)
        return c

    for c in loads:
        c.wait()
    pl.semaphore_wait(barrier, 4)

    hops = {}

    def pass_on(piece, slot, way=None):
        buf, path = ((qbuf, Q_PATH), (gbuf, G_PATH))[piece // 2]
        half = piece % 2
        for src, dst, steps in path:
            if src == slot and way in (None, steps > 0):
                n = piece * 8 + dst
                hops[piece, dst] = send(
                    buf.at[half, src], buf.at[half, dst], gat_send.at[n], gat_recv.at[n], on_ring(steps)
                )

    def arrive(piece, slot):
        hops[piece, slot].wait_recv()
        pass_on(piece, slot)

    def key_rows_at(p):
        return pl.ds(p * ROWS, ROWS)

    for a, b in PIECES:
        pass_on(a, OWN, True)
        pass_on(b, OWN, False)
    kv_across = []
    for i, buf in enumerate((kbuf, vbuf)):
        kv_across.append(
            send(buf.at[key_rows_at(0)], buf.at[key_rows_at(2)], kv_send.at[i], kv_recv.at[i], across)
        )
    kv_sibling = []
    for i, buf in enumerate((kbuf, vbuf)):
        kv_sibling.append(
            send(buf.at[key_rows_at(0)], buf.at[key_rows_at(1)], kv_send.at[2 + i], kv_recv.at[2 + i], sibling)
        )
    kv_third = []

    def pass_keys_on():
        for i, buf in enumerate((kbuf, vbuf)):
            kv_across[i].wait_recv()
            kv_third.append(
                send(buf.at[key_rows_at(2)], buf.at[key_rows_at(3)], kv_send.at[4 + i], kv_recv.at[4 + i], sibling)
            )

    def side_by_side(buf, half, pair):
        return buf[half, 2 * pair : 2 * pair + 2].reshape(2 * PART, WIDTH)

    def tile(half, pair, side=None):
        t = half * 4 + pair
        if side is None:
            cols, slots = slice(0, 2 * PART), (2 * pair, 2 * pair + 1)
            queries, grads_out = side_by_side(qbuf, half, pair), side_by_side(gbuf, half, pair)
        else:
            cols, slots = slice(side * PART, side * PART + PART), (2 * pair + side,)
            queries, grads_out = qbuf[half, slots[0]], gbuf[half, slots[0]]
        for kh in (0, 1):
            keys = pl.ds(kh * HALF, HALF)
            s = rows_dot(kbuf[keys, :], queries)
            m = jnp.max(s, axis=0, keepdims=True)
            e = jnp.exp2((s - m) * EXP2_SCALE)
            ebuf[t, keys, cols] = e
            d = rows_dot(vbuf[keys, :], grads_out)
            dbuf[t, keys, cols] = d
            mbuf[t, kh, 0:1, cols] = m * SCALE
            mbuf[t, kh, 1:2, cols] = jnp.sum(e, axis=0, keepdims=True)
            mbuf[t, kh, 2:3, cols] = jnp.sum(e * d, axis=0, keepdims=True)
        m0, l0, w0 = (mbuf[t, 0, i : i + 1, cols] for i in range(3))
        m1, l1, w1 = (mbuf[t, 1, i : i + 1, cols] for i in range(3))
        m = jnp.maximum(m0, m1)
        a0, a1 = jnp.exp(m0 - m), jnp.exp(m1 - m)
        total = l0 * a0 + l1 * a1
        log_total = m + jnp.log(total)
        delta = (w0 * a0 + w1 * a1) / total
        for i, slot in enumerate(slots):
            part_tx[half, slot, 0:1, :] = log_total[:, i * PART : (i + 1) * PART]
            part_tx[half, slot, 1:2, :] = delta[:, i * PART : (i + 1) * PART]

    st = {}

    def share_stats(half, g):
        group = pl.ds(g * 4, 4)
        n = half * 2 + g
        for slot in PEERS:
            at = MIRROR[slot]
            st[at, half, g] = send(
                part_tx.at[half, group], part_rx.at[at, half, group],
                st_send.at[slot, n], st_recv.at[at, n], on_ring(PLACE[slot]),
            )

    def parts_of(half, t, g):
        found = []
        for u in range(8):
            s = SLOT_AT[(PLACE[t] - PLACE[u]) % RING]
            if s // 4 == g:
                ref = part_tx if u == OWN else part_rx.at[u]
                found.append((ref[half, s, 0:1, :], ref[half, s, 1:2, :]))
        return found

    def combine(parts):
        peak = parts[0][0]
        for part in parts[1:]:
            peak = jnp.maximum(peak, part[0])
        total = jnp.zeros_like(peak)
        weighted = jnp.zeros_like(peak)
        for log_part, delta_part in parts:
            share = jnp.exp(log_part - peak)
            total = total + share
            weighted = weighted + share * delta_part
        return peak + jnp.log(total), weighted / total

    partial = {}

    def early_stats(half):
        for slot in PEERS:
            st[slot, half, 0].wait_recv()
        for slot in range(8):
            partial[half, slot] = combine(parts_of(half, slot, 0))

    def late_stats(half):
        for slot in PEERS:
            st[slot, half, 1].wait_recv()

    rows_stats = {}

    def grads(half, pair, kh):
        t = half * 4 + pair
        if t not in rows_stats:
            both = [combine([partial[half, x]] + parts_of(half, x, 1)) for x in (2 * pair, 2 * pair + 1)]
            rows_stats[t] = tuple(jnp.concatenate(x, axis=1) for x in zip(*both))
        log_total, delta = rows_stats[t]
        keys = pl.ds(kh * HALF, HALF)
        c = jnp.exp(mbuf[t, kh, 0:1, :] - log_total)
        p = ebuf[t, keys, :] * c
        prob_half = p.astype(BF16)
        score_grad = (p * (dbuf[t, keys, :] - delta)).astype(BF16)
        dv = jnp.dot(prob_half, side_by_side(gbuf, half, pair), preferred_element_type=F32)
        dk = jnp.dot(score_grad, side_by_side(qbuf, half, pair), preferred_element_type=F32)
        if (half, pair) == (0, R3 // 2):
            dv_acc[keys, :] = dv
            dk_acc[keys, :] = dk
        else:
            dv_acc[keys, :] += dv
            dk_acc[keys, :] += dk
        return jnp.dot(ktbuf[:, keys], score_grad, preferred_element_type=F32)

    dq = {}
    sides = (slice(0, PART), slice(PART, 2 * PART))
    own_sum, far_sum = (0, 5), (1, 3)

    def send_sum(half, d, kind, value):
        n = (half * 2 + d) * 4 + kind
        dq_tx[n] = value.astype(BF16)
        steps = (4, 1, 2, 1)[kind]
        dq[half, d, kind] = send(
            dq_tx.at[n], dq_rx.at[n], dq_send.at[n], dq_recv.at[n], on_ring(steps if d else -steps)
        )

    def received(half, d, kind):
        dq[half, d, kind].wait_recv()
        return dq_rx[(half * 2 + d) * 4 + kind].astype(F32)

    def send_both(half, kind, value):
        for d in (0, 1):
            send_sum(half, d, kind, value[:, sides[d]])

    def far_sums(half):
        for d in (0, 1):
            send_sum(half, d, 2, dqt[far_sum[half], :, sides[d]] + received(half, d, 1))

    for a, b in PIECES:
        arrive(a, R1)
        arrive(b, L1)
    pass_keys_on()
    for a, b in PIECES[:2]:
        arrive(a, R2)
        arrive(b, L2)
    for c in kv_sibling + kv_third:
        c.wait_recv()
    tile(0, 3, 0)
    tile(0, 0)
    for a, b in PIECES[2:]:
        arrive(a, R2)
        arrive(b, L2)
    tile(0, 1)
    tile(1, 3, 0)
    tile(1, 0)
    for p in range(4):
        ktbuf[:, p * ROWS : (p + 1) * ROWS] = kbuf[key_rows_at(p), :].astype(F32).T.astype(BF16)
    for half in (0, 1):
        for piece in (half, 2 + half):
            arrive(piece, R3)
            arrive(piece, L3)
        if half == 0:
            share_stats(0, 0)
        tile(half, 2)
        for piece in (half, 2 + half):
            arrive(piece, FAR)
        tile(half, 3, 1)
        share_stats(half, 1)
        if half == 0:
            tile(1, 1)
            share_stats(1, 0)

    early_stats(0)
    late_stats(0)
    send_both(0, 1, grads(0, 2, 0) + grads(0, 2, 1))
    t = grads(0, 3, 0) + grads(0, 3, 1)
    send_sum(0, 0, 0, t[:, sides[1]])
    dqt[0, :, sides[0]] = t[:, sides[0]]
    dqt[1] = grads(0, 1, 0) + grads(0, 1, 1)
    send_both(0, 3, grads(0, 0, 0) + grads(0, 0, 1))

    early_stats(1)
    late_stats(1)
    dqt[4] = grads(1, 2, 1)
    for pair in (3, 1, 0):
        dqt[2 + pair] = grads(1, pair, 1)
    accs = (dk_acc, dv_acc)
    pair_sum = {}
    across_sum = []

    def send_pair(j, p):
        for i, acc in enumerate(accs):
            n = j * 2 + i
            pair_tx[n] = acc[key_rows_at(p), :].astype(BF16)
            pair_sum[j, i] = send(pair_tx.at[n], pair_rx.at[n], red_send.at[n], red_recv.at[n], sibling)

    def from_pair(j, i):
        pair_sum[j, i].wait_recv()
        return pair_rx[j * 2 + i].astype(F32)

    send_pair(0, 3)
    send_both(1, 1, dqt[4] + grads(1, 2, 0))
    t = dqt[5] + grads(1, 3, 0)
    send_sum(1, 0, 0, t[:, sides[1]])
    dqt[5, :, sides[0]] = t[:, sides[0]]
    far_sums(0)
    dqt[3] += grads(1, 1, 0)
    for i, acc in enumerate(accs):
        far_tx[i] = (acc[key_rows_at(2), :] + from_pair(0, i)).astype(BF16)
        across_sum.append(
            send(far_tx.at[i], far_rx.at[i], red_send.at[4 + i], red_recv.at[4 + i], across)
        )
    send_both(1, 3, dqt[2] + grads(1, 0, 0))
    send_pair(1, 1)
    far_sums(1)

    for half in (0, 1):
        t = dqt[own_sum[half], :, sides[0]] + received(half, 0, 0)
        for d in (0, 1):
            t = t + received(half, d, 3)
        if half == 0:
            for d in (0, 1):
                t = t + received(half, d, 2)
            dq_out[0:PART, :] = t.T * SCALE
        else:
            dqt[5, :, sides[0]] = t
    for i, (acc, out, scale) in enumerate(((dk_acc, dk_out, SCALE), (dv_acc, dv_out, None))):
        t = acc[key_rows_at(0), :] + from_pair(1, i)
        across_sum[i].wait_recv()
        t = t + far_rx[i].astype(F32)
        out[...] = t if scale is None else t * scale
    t = dqt[5, :, sides[0]]
    for d in (0, 1):
        t = t + received(1, d, 2)
    dq_out[PART : 2 * PART, :] = t.T * SCALE
    for c in pending:
        c.wait_send()


def write_out(a_ref, b_ref, c_ref, a_out, b_out, c_out, sems):
    copies = [
        pltpu.make_async_copy(src, dst, sems.at[i])
        for i, (src, dst) in enumerate(((a_ref, a_out), (b_ref, b_out), (c_ref, c_out)))
    ]
    for c in copies:
        c.start()
    for c in copies:
        c.wait()


def shards(queries, key_rows, value_rows, out_grad):
    any_spec = pl.BlockSpec(memory_space=pl.ANY)
    dma = pltpu.SemaphoreType.DMA
    out = jax.ShapeDtypeStruct((ROWS, WIDTH), F32)
    near = pltpu.VMEM((ROWS, WIDTH), F32)
    near_spec = pl.BlockSpec(memory_space=pltpu.VMEM)
    vm = pltpu.VMEM
    grads = pl.pallas_call(
        kernel,
        out_shape=(near, near, near),
        in_specs=[any_spec] * 4,
        out_specs=(near_spec,) * 3,
        scratch_shapes=[
            vm((2, 8, PART, WIDTH), BF16),
            vm((2, 8, PART, WIDTH), BF16),
            vm((KEYS, WIDTH), BF16),
            vm((KEYS, WIDTH), BF16),
            vm((WIDTH, KEYS), BF16),
            vm((8, KEYS, ROWS), F32),
            vm((8, KEYS, ROWS), F32),
            vm((8, 2, 8, ROWS), F32),
            vm((2, 8, 2, PART), F32),
            vm((8, 2, 8, 2, PART), F32),
            vm((KEYS, WIDTH), F32),
            vm((KEYS, WIDTH), F32),
            vm((6, WIDTH, 2 * PART), F32),
            vm((16, WIDTH, PART), BF16),
            vm((16, WIDTH, PART), BF16),
            vm((4, ROWS, WIDTH), BF16),
            vm((4, ROWS, WIDTH), BF16),
            vm((2, ROWS, WIDTH), BF16),
            vm((2, ROWS, WIDTH), BF16),
            dma((6,)),
            dma((32,)),
            dma((32,)),
            dma((6,)),
            dma((6,)),
            dma((8, 4)),
            dma((8, 4)),
            dma((16,)),
            dma((16,)),
            dma((6,)),
            dma((6,)),
        ],
        compiler_params=pltpu.CompilerParams(
            collective_id=0, has_side_effects=True, vmem_limit_bytes=56 * 1024 * 1024
        ),
        cost_estimate=pl.CostEstimate(
            flops=2 * 5 * KEYS * 8 * ROWS * WIDTH,
            bytes_accessed=4 * ROWS * WIDTH * 2 + 3 * ROWS * WIDTH * 4,
            transcendentals=KEYS * 8 * ROWS,
        ),
    )(queries, key_rows, value_rows, out_grad)
    return pl.pallas_call(
        write_out,
        out_shape=(out, out, out),
        in_specs=[near_spec] * 3,
        out_specs=(any_spec,) * 3,
        scratch_shapes=[dma((3,))],
        compiler_params=pltpu.CompilerParams(vmem_limit_bytes=1024*1024),
    )(*grads)


def solution(mesh):
    spec = P(("dp", "ctx"), None)
    return jax.shard_map(
        shards, mesh=mesh, in_specs=(spec,) * 4, out_specs=(spec,) * 3, check_vma=False
    )
```

```python
import math

import jax
import jax.numpy as jnp
from jax import lax
from jax.experimental import pallas as pl
from jax.experimental.pallas import tpu as pltpu
from jax.sharding import PartitionSpec as P

F32 = jnp.float32
BF16 = jnp.bfloat16
MESH = pl.DeviceIdType.MESH

ROWS = 256
WIDTH = 128
RING = 8
HALF = 512
KEYS = 1024
SCALE = WIDTH ** (-0.5)
EXP2_SCALE = SCALE * math.log2(math.e)

R1, L1, R2, L2, R3, L3, OWN, FAR = range(8)
PLACE = (-1, 1, -2, 2, -3, 3, 0, 4)
SLOT_AT = {p % RING: s for s, p in enumerate(PLACE)}
MIRROR = tuple(SLOT_AT[-p % RING] for p in PLACE)
PEERS = (FAR, R3, L3, R2, L2, R1, L1)
PART = 128

Q_PATH = ((OWN, R1, 1), (OWN, L1, -1), (R1, R2, 1), (L1, L2, -1), (R2, FAR, 2), (R2, R3, 1), (L2, L3, -1))
G_PATH = ((OWN, R1, 1), (OWN, L1, -1), (R1, R2, 1), (L1, L2, -1), (L2, FAR, -2), (R2, R3, 1), (L2, L3, -1))
PIECES = ((0, 2), (2, 0), (1, 3), (3, 1))


def rows_dot(left, right):
    return lax.dot_general(left, right, (((1,), (1,)), ((), ())), preferred_element_type=F32)


def kernel(
    q_hbm, k_hbm, v_hbm, g_hbm,
    dq_out, dk_out, dv_out,
    qbuf, gbuf, kbuf, vbuf, ktbuf, ebuf, dbuf, mbuf,
    part_tx, part_rx, dk_acc, dv_acc,
    dqt, dq_tx, dq_rx, pair_tx, pair_rx, far_tx, far_rx,
    in_sem, gat_send, gat_recv, kv_send, kv_recv, st_send, st_recv,
    dq_send, dq_recv, red_send, red_recv,
):
    me = lax.axis_index("ctx")
    z = me // 4
    w = me % 4
    core = w % 2
    xh = w // 2

    def on_ring(offset):
        return {"ctx": ((z + (offset + RING)) % RING) * 4 + w}

    sibling = {"ctx": z * 4 + xh * 2 + (1 - core)}
    across = {"ctx": z * 4 + (1 - xh) * 2 + core}
    right, left = on_ring(1), on_ring(-1)

    barrier = pltpu.get_barrier_semaphore()
    for peer in (right, left, across, sibling):
        pl.semaphore_signal(barrier, inc=1, device_id=peer, device_id_type=MESH)

    own_rows = pl.ds(0, ROWS)
    loads = [
        pltpu.make_async_copy(src, dst, in_sem.at[i])
        for i, (src, dst) in enumerate(
            (
                (q_hbm.at[pl.ds(0, PART)], qbuf.at[0, OWN]),
                (g_hbm.at[pl.ds(0, PART)], gbuf.at[0, OWN]),
                (q_hbm.at[pl.ds(PART, PART)], qbuf.at[1, OWN]),
                (g_hbm.at[pl.ds(PART, PART)], gbuf.at[1, OWN]),
                (k_hbm, kbuf.at[own_rows]),
                (v_hbm, vbuf.at[own_rows]),
            )
        )
    ]
    for c in loads:
        c.start()
    pending = []

    def send(src, dst, send_sem, recv_sem, peer):
        c = pltpu.make_async_remote_copy(
            src_ref=src, dst_ref=dst, send_sem=send_sem, recv_sem=recv_sem,
            device_id=peer, device_id_type=MESH,
        )
        c.start()
        pending.append(c)
        return c

    for c in loads:
        c.wait()
    pl.semaphore_wait(barrier, 4)

    hops = {}

    def pass_on(piece, slot, way=None):
        buf, path = ((qbuf, Q_PATH), (gbuf, G_PATH))[piece // 2]
        half = piece % 2
        for src, dst, steps in path:
            if src == slot and way in (None, steps > 0):
                n = piece * 8 + dst
                hops[piece, dst] = send(
                    buf.at[half, src], buf.at[half, dst], gat_send.at[n], gat_recv.at[n], on_ring(steps)
                )

    def arrive(piece, slot):
        hops[piece, slot].wait_recv()
        pass_on(piece, slot)

    def key_rows_at(p):
        return pl.ds(p * ROWS, ROWS)

    for a, b in PIECES:
        pass_on(a, OWN, True)
        pass_on(b, OWN, False)
    kv_across = []
    for i, buf in enumerate((kbuf, vbuf)):
        kv_across.append(
            send(buf.at[key_rows_at(0)], buf.at[key_rows_at(2)], kv_send.at[i], kv_recv.at[i], across)
        )
    kv_sibling = []
    for i, buf in enumerate((kbuf, vbuf)):
        kv_sibling.append(
            send(buf.at[key_rows_at(0)], buf.at[key_rows_at(1)], kv_send.at[2 + i], kv_recv.at[2 + i], sibling)
        )
    kv_third = []

    def pass_keys_on():
        for i, buf in enumerate((kbuf, vbuf)):
            kv_across[i].wait_recv()
            kv_third.append(
                send(buf.at[key_rows_at(2)], buf.at[key_rows_at(3)], kv_send.at[4 + i], kv_recv.at[4 + i], sibling)
            )

    def side_by_side(buf, half, pair):
        return buf[half, 2 * pair : 2 * pair + 2].reshape(2 * PART, WIDTH)

    def tile(half, pair, side=None):
        t = half * 4 + pair
        if side is None:
            cols, slots = slice(0, 2 * PART), (2 * pair, 2 * pair + 1)
            queries, grads_out = side_by_side(qbuf, half, pair), side_by_side(gbuf, half, pair)
        else:
            cols, slots = slice(side * PART, side * PART + PART), (2 * pair + side,)
            queries, grads_out = qbuf[half, slots[0]], gbuf[half, slots[0]]
        for kh in (0, 1):
            keys = pl.ds(kh * HALF, HALF)
            s = rows_dot(kbuf[keys, :], queries)
            m = jnp.max(s, axis=0, keepdims=True)
            e = jnp.exp2((s - m) * EXP2_SCALE)
            ebuf[t, keys, cols] = e
            d = rows_dot(vbuf[keys, :], grads_out)
            dbuf[t, keys, cols] = d
            mbuf[t, kh, 0:1, cols] = m * SCALE
            mbuf[t, kh, 1:2, cols] = jnp.sum(e, axis=0, keepdims=True)
            mbuf[t, kh, 2:3, cols] = jnp.sum(e * d, axis=0, keepdims=True)
        m0, l0, w0 = (mbuf[t, 0, i : i + 1, cols] for i in range(3))
        m1, l1, w1 = (mbuf[t, 1, i : i + 1, cols] for i in range(3))
        m = jnp.maximum(m0, m1)
        a0, a1 = jnp.exp(m0 - m), jnp.exp(m1 - m)
        total = l0 * a0 + l1 * a1
        log_total = m + jnp.log(total)
        delta = (w0 * a0 + w1 * a1) / total
        for i, slot in enumerate(slots):
            part_tx[half, slot, 0:1, :] = log_total[:, i * PART : (i + 1) * PART]
            part_tx[half, slot, 1:2, :] = delta[:, i * PART : (i + 1) * PART]

    st = {}

    def share_stats(half, g):
        group = pl.ds(g * 4, 4)
        n = half * 2 + g
        for slot in PEERS:
            at = MIRROR[slot]
            st[at, half, g] = send(
                part_tx.at[half, group], part_rx.at[at, half, group],
                st_send.at[slot, n], st_recv.at[at, n], on_ring(PLACE[slot]),
            )

    def parts_of(half, t, g):
        found = []
        for u in range(8):
            s = SLOT_AT[(PLACE[t] - PLACE[u]) % RING]
            if s // 4 == g:
                ref = part_tx if u == OWN else part_rx.at[u]
                found.append((ref[half, s, 0:1, :], ref[half, s, 1:2, :]))
        return found

    def combine(parts):
        peak = parts[0][0]
        for part in parts[1:]:
            peak = jnp.maximum(peak, part[0])
        total = jnp.zeros_like(peak)
        weighted = jnp.zeros_like(peak)
        for log_part, delta_part in parts:
            share = jnp.exp(log_part - peak)
            total = total + share
            weighted = weighted + share * delta_part
        return peak + jnp.log(total), weighted / total

    partial = {}

    def early_stats(half):
        for slot in PEERS:
            st[slot, half, 0].wait_recv()
        for slot in range(8):
            partial[half, slot] = combine(parts_of(half, slot, 0))

    def late_stats(half):
        for slot in PEERS:
            st[slot, half, 1].wait_recv()

    rows_stats = {}

    def grads(half, pair, kh):
        t = half * 4 + pair
        if t not in rows_stats:
            both = [combine([partial[half, x]] + parts_of(half, x, 1)) for x in (2 * pair, 2 * pair + 1)]
            rows_stats[t] = tuple(jnp.concatenate(x, axis=1) for x in zip(*both))
        log_total, delta = rows_stats[t]
        keys = pl.ds(kh * HALF, HALF)
        c = jnp.exp(mbuf[t, kh, 0:1, :] - log_total)
        p = ebuf[t, keys, :] * c
        prob_half = p.astype(BF16)
        score_grad = (p * (dbuf[t, keys, :] - delta)).astype(BF16)
        dv = jnp.dot(prob_half, side_by_side(gbuf, half, pair), preferred_element_type=F32)
        dk = jnp.dot(score_grad, side_by_side(qbuf, half, pair), preferred_element_type=F32)
        if (half, pair) == (0, R3 // 2):
            dv_acc[keys, :] = dv
            dk_acc[keys, :] = dk
        else:
            dv_acc[keys, :] += dv
            dk_acc[keys, :] += dk
        return jnp.dot(ktbuf[:, keys], score_grad, preferred_element_type=F32)

    dq = {}
    sides = (slice(0, PART), slice(PART, 2 * PART))
    own_sum, far_sum = (0, 5), (1, 3)

    def send_sum(half, d, kind, value):
        n = (half * 2 + d) * 4 + kind
        dq_tx[n] = value.astype(BF16)
        steps = (4, 1, 2, 1)[kind]
        dq[half, d, kind] = send(
            dq_tx.at[n], dq_rx.at[n], dq_send.at[n], dq_recv.at[n], on_ring(steps if d else -steps)
        )

    def received(half, d, kind):
        dq[half, d, kind].wait_recv()
        return dq_rx[(half * 2 + d) * 4 + kind].astype(F32)

    def send_both(half, kind, value):
        for d in (0, 1):
            send_sum(half, d, kind, value[:, sides[d]])

    def far_sums(half):
        for d in (0, 1):
            send_sum(half, d, 2, dqt[far_sum[half], :, sides[d]] + received(half, d, 1))

    for a, b in PIECES:
        arrive(a, R1)
        arrive(b, L1)
    pass_keys_on()
    for a, b in PIECES[:2]:
        arrive(a, R2)
        arrive(b, L2)
    for c in kv_sibling + kv_third:
        c.wait_recv()
    tile(0, 3, 0)
    tile(0, 0)
    for a, b in PIECES[2:]:
        arrive(a, R2)
        arrive(b, L2)
    tile(0, 1)
    tile(1, 3, 0)
    tile(1, 0)
    for half in (0, 1):
        for piece in (half, 2 + half):
            arrive(piece, R3)
            arrive(piece, L3)
        if half == 0:
            share_stats(0, 0)
        tile(half, 2)
        for piece in (half, 2 + half):
            arrive(piece, FAR)
        tile(half, 3, 1)
        share_stats(half, 1)
        if half == 0:
            tile(1, 1)
            share_stats(1, 0)

    for p in range(4):
        ktbuf[:, p * ROWS : (p + 1) * ROWS] = kbuf[key_rows_at(p), :].astype(F32).T.astype(BF16)
    early_stats(0)
    late_stats(0)
    send_both(0, 1, grads(0, 2, 0) + grads(0, 2, 1))
    t = grads(0, 3, 0) + grads(0, 3, 1)
    send_sum(0, 0, 0, t[:, sides[1]])
    dqt[0, :, sides[0]] = t[:, sides[0]]
    dqt[1] = grads(0, 1, 0) + grads(0, 1, 1)
    send_both(0, 3, grads(0, 0, 0) + grads(0, 0, 1))

    early_stats(1)
    late_stats(1)
    dqt[4] = grads(1, 2, 1)
    for pair in (3, 1, 0):
        dqt[2 + pair] = grads(1, pair, 1)
    accs = (dk_acc, dv_acc)
    pair_sum = {}
    across_sum = []

    def send_pair(j, p):
        for i, acc in enumerate(accs):
            n = j * 2 + i
            pair_tx[n] = acc[key_rows_at(p), :].astype(BF16)
            pair_sum[j, i] = send(pair_tx.at[n], pair_rx.at[n], red_send.at[n], red_recv.at[n], sibling)

    def from_pair(j, i):
        pair_sum[j, i].wait_recv()
        return pair_rx[j * 2 + i].astype(F32)

    send_pair(0, 3)
    send_both(1, 1, dqt[4] + grads(1, 2, 0))
    t = dqt[5] + grads(1, 3, 0)
    send_sum(1, 0, 0, t[:, sides[1]])
    dqt[5, :, sides[0]] = t[:, sides[0]]
    far_sums(0)
    dqt[3] += grads(1, 1, 0)
    for i, acc in enumerate(accs):
        far_tx[i] = (acc[key_rows_at(2), :] + from_pair(0, i)).astype(BF16)
        across_sum.append(
            send(far_tx.at[i], far_rx.at[i], red_send.at[4 + i], red_recv.at[4 + i], across)
        )
    send_both(1, 3, dqt[2] + grads(1, 0, 0))
    send_pair(1, 1)
    far_sums(1)

    for half in (0, 1):
        t = dqt[own_sum[half], :, sides[0]] + received(half, 0, 0)
        for d in (0, 1):
            t = t + received(half, d, 3)
        if half == 0:
            for d in (0, 1):
                t = t + received(half, d, 2)
            dq_out[0:PART, :] = t.T * SCALE
        else:
            dqt[5, :, sides[0]] = t
    for i, (acc, out, scale) in enumerate(((dk_acc, dk_out, SCALE), (dv_acc, dv_out, None))):
        t = acc[key_rows_at(0), :] + from_pair(1, i)
        across_sum[i].wait_recv()
        t = t + far_rx[i].astype(F32)
        out[...] = t if scale is None else t * scale
    t = dqt[5, :, sides[0]]
    for d in (0, 1):
        t = t + received(1, d, 2)
    dq_out[PART : 2 * PART, :] = t.T * SCALE
    for c in pending:
        c.wait_send()


def write_out(a_ref, b_ref, c_ref, a_out, b_out, c_out, sems):
    copies = [
        pltpu.make_async_copy(src, dst, sems.at[i])
        for i, (src, dst) in enumerate(((a_ref, a_out), (b_ref, b_out), (c_ref, c_out)))
    ]
    for c in copies:
        c.start()
    for c in copies:
        c.wait()


def shards(queries, key_rows, value_rows, out_grad):
    any_spec = pl.BlockSpec(memory_space=pl.ANY)
    dma = pltpu.SemaphoreType.DMA
    out = jax.ShapeDtypeStruct((ROWS, WIDTH), F32)
    near = pltpu.VMEM((ROWS, WIDTH), F32)
    near_spec = pl.BlockSpec(memory_space=pltpu.VMEM)
    vm = pltpu.VMEM
    grads = pl.pallas_call(
        kernel,
        out_shape=(near, near, near),
        in_specs=[any_spec] * 4,
        out_specs=(near_spec,) * 3,
        scratch_shapes=[
            vm((2, 8, PART, WIDTH), BF16),
            vm((2, 8, PART, WIDTH), BF16),
            vm((KEYS, WIDTH), BF16),
            vm((KEYS, WIDTH), BF16),
            vm((WIDTH, KEYS), BF16),
            vm((8, KEYS, ROWS), F32),
            vm((8, KEYS, ROWS), F32),
            vm((8, 2, 8, ROWS), F32),
            vm((2, 8, 2, PART), F32),
            vm((8, 2, 8, 2, PART), F32),
            vm((KEYS, WIDTH), F32),
            vm((KEYS, WIDTH), F32),
            vm((6, WIDTH, 2 * PART), F32),
            vm((16, WIDTH, PART), BF16),
            vm((16, WIDTH, PART), BF16),
            vm((4, ROWS, WIDTH), BF16),
            vm((4, ROWS, WIDTH), BF16),
            vm((2, ROWS, WIDTH), BF16),
            vm((2, ROWS, WIDTH), BF16),
            dma((6,)),
            dma((32,)),
            dma((32,)),
            dma((6,)),
            dma((6,)),
            dma((8, 4)),
            dma((8, 4)),
            dma((16,)),
            dma((16,)),
            dma((6,)),
            dma((6,)),
        ],
        compiler_params=pltpu.CompilerParams(
            collective_id=0, has_side_effects=True, vmem_limit_bytes=56 * 1024 * 1024
        ),
        cost_estimate=pl.CostEstimate(
            flops=2 * 5 * KEYS * 8 * ROWS * WIDTH,
            bytes_accessed=4 * ROWS * WIDTH * 2 + 3 * ROWS * WIDTH * 4,
            transcendentals=KEYS * 8 * ROWS,
        ),
    )(queries, key_rows, value_rows, out_grad)
    return pl.pallas_call(
        write_out,
        out_shape=(out, out, out),
        in_specs=[near_spec] * 3,
        out_specs=(any_spec,) * 3,
        scratch_shapes=[dma((3,))],
        compiler_params=pltpu.CompilerParams(vmem_limit_bytes=1024*1024),
    )(*grads)


def solution(mesh):
    spec = P(("dp", "ctx"), None)
    return jax.shard_map(
        shards, mesh=mesh, in_specs=(spec,) * 4, out_specs=(spec,) * 3, check_vma=False
    )
```

```python
import math

import jax
import jax.numpy as jnp
from jax import lax
from jax.experimental import pallas as pl
from jax.experimental.pallas import tpu as pltpu
from jax.sharding import PartitionSpec as P

F32 = jnp.float32
BF16 = jnp.bfloat16
MESH = pl.DeviceIdType.MESH

ROWS = 256
WIDTH = 128
RING = 8
HALF = 512
KEYS = 1024
SCALE = WIDTH ** (-0.5)
EXP2_SCALE = SCALE * math.log2(math.e)

R1, L1, R2, L2, R3, L3, OWN, FAR = range(8)
PLACE = (-1, 1, -2, 2, -3, 3, 0, 4)
SLOT_AT = {p % RING: s for s, p in enumerate(PLACE)}
MIRROR = tuple(SLOT_AT[-p % RING] for p in PLACE)
PEERS = (FAR, R3, L3, R2, L2, R1, L1)
PART = 128

Q_PATH = ((OWN, R1, 1), (OWN, L1, -1), (R1, R2, 1), (L1, L2, -1), (R2, FAR, 2), (R2, R3, 1), (L2, L3, -1))
G_PATH = ((OWN, R1, 1), (OWN, L1, -1), (R1, R2, 1), (L1, L2, -1), (L2, FAR, -2), (R2, R3, 1), (L2, L3, -1))
PIECES = ((0, 2), (2, 0), (1, 3), (3, 1))


def rows_dot(left, right):
    return lax.dot_general(left, right, (((1,), (1,)), ((), ())), preferred_element_type=F32)


def kernel(
    q_hbm, k_hbm, v_hbm, g_hbm,
    dq_out, dk_out, dv_out,
    qbuf, gbuf, kbuf, vbuf, ktbuf, ebuf, dbuf, mbuf,
    part_tx, part_rx, dk_acc, dv_acc,
    dqt, dq_tx, dq_rx, pair_tx, pair_rx, far_tx, far_rx,
    in_sem, gat_send, gat_recv, kv_send, kv_recv, st_send, st_recv,
    dq_send, dq_recv, red_send, red_recv,
):
    me = lax.axis_index("ctx")
    z = me // 4
    w = me % 4
    core = w % 2
    xh = w // 2

    def on_ring(offset):
        return {"ctx": ((z + (offset + RING)) % RING) * 4 + w}

    sibling = {"ctx": z * 4 + xh * 2 + (1 - core)}
    across = {"ctx": z * 4 + (1 - xh) * 2 + core}
    right, left = on_ring(1), on_ring(-1)

    barrier = pltpu.get_barrier_semaphore()
    for peer in (right, left, across, sibling):
        pl.semaphore_signal(barrier, inc=1, device_id=peer, device_id_type=MESH)

    own_rows = pl.ds(0, ROWS)
    loads = [
        pltpu.make_async_copy(src, dst, in_sem.at[i])
        for i, (src, dst) in enumerate(
            (
                (q_hbm.at[pl.ds(0, PART)], qbuf.at[0, OWN]),
                (g_hbm.at[pl.ds(0, PART)], gbuf.at[0, OWN]),
                (q_hbm.at[pl.ds(PART, PART)], qbuf.at[1, OWN]),
                (g_hbm.at[pl.ds(PART, PART)], gbuf.at[1, OWN]),
                (k_hbm, kbuf.at[own_rows]),
                (v_hbm, vbuf.at[own_rows]),
            )
        )
    ]
    for c in loads:
        c.start()
    pending = []

    def send(src, dst, send_sem, recv_sem, peer):
        c = pltpu.make_async_remote_copy(
            src_ref=src, dst_ref=dst, send_sem=send_sem, recv_sem=recv_sem,
            device_id=peer, device_id_type=MESH,
        )
        c.start()
        pending.append(c)
        return c

    for c in loads:
        c.wait()
    pl.semaphore_wait(barrier, 4)

    hops = {}

    def pass_on(piece, slot, way=None):
        buf, path = ((qbuf, Q_PATH), (gbuf, G_PATH))[piece // 2]
        half = piece % 2
        for src, dst, steps in path:
            if src == slot and way in (None, steps > 0):
                n = piece * 8 + dst
                hops[piece, dst] = send(
                    buf.at[half, src], buf.at[half, dst], gat_send.at[n], gat_recv.at[n], on_ring(steps)
                )

    def arrive(piece, slot):
        hops[piece, slot].wait_recv()
        pass_on(piece, slot)

    def key_rows_at(p):
        return pl.ds(p * ROWS, ROWS)

    for a, b in PIECES:
        pass_on(a, OWN, True)
        pass_on(b, OWN, False)
    kv_across = []
    for i, buf in enumerate((kbuf, vbuf)):
        kv_across.append(
            send(buf.at[key_rows_at(0)], buf.at[key_rows_at(2)], kv_send.at[i], kv_recv.at[i], across)
        )
    kv_sibling = []
    for i, buf in enumerate((kbuf, vbuf)):
        kv_sibling.append(
            send(buf.at[key_rows_at(0)], buf.at[key_rows_at(1)], kv_send.at[2 + i], kv_recv.at[2 + i], sibling)
        )
    kv_third = []

    def pass_keys_on():
        for i, buf in enumerate((kbuf, vbuf)):
            kv_across[i].wait_recv()
            kv_third.append(
                send(buf.at[key_rows_at(2)], buf.at[key_rows_at(3)], kv_send.at[4 + i], kv_recv.at[4 + i], sibling)
            )

    def side_by_side(buf, half, pair):
        return buf[half, 2 * pair : 2 * pair + 2].reshape(2 * PART, WIDTH)

    def tile(half, pair, side=None):
        t = half * 4 + pair
        if side is None:
            cols, slots = slice(0, 2 * PART), (2 * pair, 2 * pair + 1)
            queries, grads_out = side_by_side(qbuf, half, pair), side_by_side(gbuf, half, pair)
        else:
            cols, slots = slice(side * PART, side * PART + PART), (2 * pair + side,)
            queries, grads_out = qbuf[half, slots[0]], gbuf[half, slots[0]]
        for kh in (0, 1):
            keys = pl.ds(kh * HALF, HALF)
            s = rows_dot(kbuf[keys, :], queries)
            m = jnp.max(s, axis=0, keepdims=True)
            e = jnp.exp2((s - m) * EXP2_SCALE)
            ebuf[t, keys, cols] = e
            d = rows_dot(vbuf[keys, :], grads_out)
            dbuf[t, keys, cols] = d
            mbuf[t, kh, 0:1, cols] = m * SCALE
            mbuf[t, kh, 1:2, cols] = jnp.sum(e, axis=0, keepdims=True)
            mbuf[t, kh, 2:3, cols] = jnp.sum(e * d, axis=0, keepdims=True)
        m0, l0, w0 = (mbuf[t, 0, i : i + 1, cols] for i in range(3))
        m1, l1, w1 = (mbuf[t, 1, i : i + 1, cols] for i in range(3))
        m = jnp.maximum(m0, m1)
        a0, a1 = jnp.exp(m0 - m), jnp.exp(m1 - m)
        total = l0 * a0 + l1 * a1
        log_total = m + jnp.log(total)
        delta = (w0 * a0 + w1 * a1) / total
        for i, slot in enumerate(slots):
            part_tx[half, slot, 0:1, :] = log_total[:, i * PART : (i + 1) * PART]
            part_tx[half, slot, 1:2, :] = delta[:, i * PART : (i + 1) * PART]

    st = {}

    def share_stats(half, g):
        group = pl.ds(g * 4, 4)
        n = half * 2 + g
        for slot in PEERS:
            at = MIRROR[slot]
            st[at, half, g] = send(
                part_tx.at[half, group], part_rx.at[at, half, group],
                st_send.at[slot, n], st_recv.at[at, n], on_ring(PLACE[slot]),
            )

    def parts_of(half, t, g):
        found = []
        for u in range(8):
            s = SLOT_AT[(PLACE[t] - PLACE[u]) % RING]
            if s // 4 == g:
                ref = part_tx if u == OWN else part_rx.at[u]
                found.append((ref[half, s, 0:1, :], ref[half, s, 1:2, :]))
        return found

    def combine(parts):
        peak = parts[0][0]
        for part in parts[1:]:
            peak = jnp.maximum(peak, part[0])
        total = jnp.zeros_like(peak)
        weighted = jnp.zeros_like(peak)
        for log_part, delta_part in parts:
            share = jnp.exp(log_part - peak)
            total = total + share
            weighted = weighted + share * delta_part
        return peak + jnp.log(total), weighted / total

    partial = {}

    def early_stats(half):
        for slot in PEERS:
            st[slot, half, 0].wait_recv()
        for slot in range(8):
            partial[half, slot] = combine(parts_of(half, slot, 0))

    def late_stats(half):
        for slot in PEERS:
            st[slot, half, 1].wait_recv()

    rows_stats = {}

    def grads(half, pair, kh):
        t = half * 4 + pair
        if t not in rows_stats:
            both = [combine([partial[half, x]] + parts_of(half, x, 1)) for x in (2 * pair, 2 * pair + 1)]
            rows_stats[t] = tuple(jnp.concatenate(x, axis=1) for x in zip(*both))
        log_total, delta = rows_stats[t]
        keys = pl.ds(kh * HALF, HALF)
        c = jnp.exp(mbuf[t, kh, 0:1, :] - log_total)
        p = ebuf[t, keys, :] * c
        prob_half = p.astype(BF16)
        score_grad = (p * (dbuf[t, keys, :] - delta)).astype(BF16)
        dv = jnp.dot(prob_half, side_by_side(gbuf, half, pair), preferred_element_type=F32)
        dk = jnp.dot(score_grad, side_by_side(qbuf, half, pair), preferred_element_type=F32)
        if (half, pair) == (0, R3 // 2):
            dv_acc[keys, :] = dv
            dk_acc[keys, :] = dk
        else:
            dv_acc[keys, :] += dv
            dk_acc[keys, :] += dk
        return jnp.dot(ktbuf[:, keys], score_grad, preferred_element_type=F32)

    dq = {}
    sides = (slice(0, PART), slice(PART, 2 * PART))
    own_sum, far_sum = (0, 5), (1, 3)

    def send_sum(half, d, kind, value):
        n = (half * 2 + d) * 4 + kind
        dq_tx[n] = value.astype(BF16)
        steps = (4, 1, 2, 1)[kind]
        dq[half, d, kind] = send(
            dq_tx.at[n], dq_rx.at[n], dq_send.at[n], dq_recv.at[n], on_ring(steps if d else -steps)
        )

    def received(half, d, kind):
        dq[half, d, kind].wait_recv()
        return dq_rx[(half * 2 + d) * 4 + kind].astype(F32)

    def send_both(half, kind, value):
        for d in (0, 1):
            send_sum(half, d, kind, value[:, sides[d]])

    def far_sums(half):
        for d in (0, 1):
            send_sum(half, d, 2, dqt[far_sum[half], :, sides[d]] + received(half, d, 1))

    for a, b in PIECES:
        arrive(a, R1)
        arrive(b, L1)
    pass_keys_on()
    for a, b in PIECES[:2]:
        arrive(a, R2)
        arrive(b, L2)
    for c in kv_sibling + kv_third:
        c.wait_recv()
    tile(0, 3, 0)
    tile(0, 0)
    for a, b in PIECES[2:]:
        arrive(a, R2)
        arrive(b, L2)
    tile(0, 1)
    tile(1, 0)
    for half in (0, 1):
        for piece in (half, 2 + half):
            arrive(piece, R3)
            arrive(piece, L3)
        if half == 0:
            share_stats(0, 0)
        tile(half, 2)
        for piece in (half, 2 + half):
            arrive(piece, FAR)
        tile(half, 3, 1)
        share_stats(half, 1)
        if half == 0:
            tile(1, 3, 0)
            tile(1, 1)
            share_stats(1, 0)

    for p in range(4):
        ktbuf[:, p * ROWS : (p + 1) * ROWS] = kbuf[key_rows_at(p), :].astype(F32).T.astype(BF16)
    early_stats(0)
    late_stats(0)
    send_both(0, 1, grads(0, 2, 0) + grads(0, 2, 1))
    t = grads(0, 3, 0) + grads(0, 3, 1)
    send_sum(0, 0, 0, t[:, sides[1]])
    dqt[0, :, sides[0]] = t[:, sides[0]]
    dqt[1] = grads(0, 1, 0) + grads(0, 1, 1)
    send_both(0, 3, grads(0, 0, 0) + grads(0, 0, 1))

    early_stats(1)
    late_stats(1)
    dqt[4] = grads(1, 2, 1)
    for pair in (3, 1, 0):
        dqt[2 + pair] = grads(1, pair, 1)
    accs = (dk_acc, dv_acc)
    pair_sum = {}
    across_sum = []

    def send_pair(j, p):
        for i, acc in enumerate(accs):
            n = j * 2 + i
            pair_tx[n] = acc[key_rows_at(p), :].astype(BF16)
            pair_sum[j, i] = send(pair_tx.at[n], pair_rx.at[n], red_send.at[n], red_recv.at[n], sibling)

    def from_pair(j, i):
        pair_sum[j, i].wait_recv()
        return pair_rx[j * 2 + i].astype(F32)

    send_pair(0, 3)
    send_both(1, 1, dqt[4] + grads(1, 2, 0))
    t = dqt[5] + grads(1, 3, 0)
    send_sum(1, 0, 0, t[:, sides[1]])
    dqt[5, :, sides[0]] = t[:, sides[0]]
    far_sums(0)
    dqt[3] += grads(1, 1, 0)
    for i, acc in enumerate(accs):
        far_tx[i] = (acc[key_rows_at(2), :] + from_pair(0, i)).astype(BF16)
        across_sum.append(
            send(far_tx.at[i], far_rx.at[i], red_send.at[4 + i], red_recv.at[4 + i], across)
        )
    send_both(1, 3, dqt[2] + grads(1, 0, 0))
    send_pair(1, 1)
    far_sums(1)

    for half in (0, 1):
        t = dqt[own_sum[half], :, sides[0]] + received(half, 0, 0)
        for d in (0, 1):
            t = t + received(half, d, 3)
        if half == 0:
            for d in (0, 1):
                t = t + received(half, d, 2)
            dq_out[0:PART, :] = t.T * SCALE
        else:
            dqt[5, :, sides[0]] = t
    for i, (acc, out, scale) in enumerate(((dk_acc, dk_out, SCALE), (dv_acc, dv_out, None))):
        t = acc[key_rows_at(0), :] + from_pair(1, i)
        across_sum[i].wait_recv()
        t = t + far_rx[i].astype(F32)
        out[...] = t if scale is None else t * scale
    t = dqt[5, :, sides[0]]
    for d in (0, 1):
        t = t + received(1, d, 2)
    dq_out[PART : 2 * PART, :] = t.T * SCALE
    for c in pending:
        c.wait_send()


def write_out(a_ref, b_ref, c_ref, a_out, b_out, c_out, sems):
    copies = [
        pltpu.make_async_copy(src, dst, sems.at[i])
        for i, (src, dst) in enumerate(((a_ref, a_out), (b_ref, b_out), (c_ref, c_out)))
    ]
    for c in copies:
        c.start()
    for c in copies:
        c.wait()


def shards(queries, key_rows, value_rows, out_grad):
    any_spec = pl.BlockSpec(memory_space=pl.ANY)
    dma = pltpu.SemaphoreType.DMA
    out = jax.ShapeDtypeStruct((ROWS, WIDTH), F32)
    near = pltpu.VMEM((ROWS, WIDTH), F32)
    near_spec = pl.BlockSpec(memory_space=pltpu.VMEM)
    vm = pltpu.VMEM
    grads = pl.pallas_call(
        kernel,
        out_shape=(near, near, near),
        in_specs=[any_spec] * 4,
        out_specs=(near_spec,) * 3,
        scratch_shapes=[
            vm((2, 8, PART, WIDTH), BF16),
            vm((2, 8, PART, WIDTH), BF16),
            vm((KEYS, WIDTH), BF16),
            vm((KEYS, WIDTH), BF16),
            vm((WIDTH, KEYS), BF16),
            vm((8, KEYS, ROWS), F32),
            vm((8, KEYS, ROWS), F32),
            vm((8, 2, 8, ROWS), F32),
            vm((2, 8, 2, PART), F32),
            vm((8, 2, 8, 2, PART), F32),
            vm((KEYS, WIDTH), F32),
            vm((KEYS, WIDTH), F32),
            vm((6, WIDTH, 2 * PART), F32),
            vm((16, WIDTH, PART), BF16),
            vm((16, WIDTH, PART), BF16),
            vm((4, ROWS, WIDTH), BF16),
            vm((4, ROWS, WIDTH), BF16),
            vm((2, ROWS, WIDTH), BF16),
            vm((2, ROWS, WIDTH), BF16),
            dma((6,)),
            dma((32,)),
            dma((32,)),
            dma((6,)),
            dma((6,)),
            dma((8, 4)),
            dma((8, 4)),
            dma((16,)),
            dma((16,)),
            dma((6,)),
            dma((6,)),
        ],
        compiler_params=pltpu.CompilerParams(
            collective_id=0, has_side_effects=True, vmem_limit_bytes=56 * 1024 * 1024
        ),
        cost_estimate=pl.CostEstimate(
            flops=2 * 5 * KEYS * 8 * ROWS * WIDTH,
            bytes_accessed=4 * ROWS * WIDTH * 2 + 3 * ROWS * WIDTH * 4,
            transcendentals=KEYS * 8 * ROWS,
        ),
    )(queries, key_rows, value_rows, out_grad)
    return pl.pallas_call(
        write_out,
        out_shape=(out, out, out),
        in_specs=[near_spec] * 3,
        out_specs=(any_spec,) * 3,
        scratch_shapes=[dma((3,))],
        compiler_params=pltpu.CompilerParams(vmem_limit_bytes=1024*1024),
    )(*grads)


def solution(mesh):
    spec = P(("dp", "ctx"), None)
    return jax.shard_map(
        shards, mesh=mesh, in_specs=(spec,) * 4, out_specs=(spec,) * 3, check_vma=False
    )
```
